128 devices in a mesh: region: 8 (over x, core), pair: 16 (over z, y).
Axes of the slice: x: 4, y: 4, z: 4, core: 2. Of those that a mesh axis runs over, the one named last changes fastest.
Arguments:
- points: float32 [3, 131072, 128], P(None, ('region', 'pair')), may hold values from -6 to 6
- offsets: float32 [3, 131072, 128], P(None, ('region', 'pair')), may hold values from -12 to 12
- normals: float32 [3, 131072, 128], P(None, ('region', 'pair')), may hold values from -6 to 6
- block_count: int32 [131072], P(('region', 'pair')), may hold values from 0 to 128, as said below
- block_edge: int32 [131072], P(('region', 'pair')), may hold values from 0 to 255
- edge_scan: int32 [32768], P(('region', 'pair')), may hold values from 0 to 127
- edge_nbr: int32 [32768], P(('region', 'pair')), may hold values from 0 to 383, as said below
- rotvec: float32 [3, 16384], P(None, ('region', 'pair')), may hold values from -0.3 to 0.3
Outputs:
- edge_pose: float32 [6, 32768], P(None, ('region', 'pair'))
- rotations: float32 [9, 16384], P(None, ('region', 'pair'))
The draws below stay inside these ranges and needn't reach their ends.
Inputs may be any that keep to these rules, and one draw needn't show every extreme that they name: `block_count`: some block is full in every draw; a count of 0 marks an empty slot. `edge_nbr`: values below 128 name a scan of the device one step lower along region, values from 256 one of the device one step higher, the rest one of the device's own scans other than the slot's own scan; devices at the ends of region name no missing neighbour.
All inputs are finite; a program needn't handle non-finite values.
Results may differ from the reference program's by a relative error of at most 0.0003.
Values sent between devices are 32-bit elements; how exact they have to be, the bound alone decides.
No kernel may reach another device: no remote copies, remote signals or barrier semaphores. Data moves between devices by JAX's collectives and lax.ppermute only.
A program may use at most 64 MiB of HBM per device.

```python
import jax
import jax.numpy as jnp
from jax import lax

PTS = 128
PSLOT = 2
SLOT = 8
SCAN_DEV = 128
SWEEPS = 2
EDGE_DEV = 256
BLOCKS = 131072
EDGES = 32768
SCANS = 16384
N_REGION = 8
N_PAIR = 16


def edge_helper(key):
    first, second, third = jax.random.split(jax.random.fold_in(key, 7), 3)
    own_scan = jax.random.randint(first, (EDGES,), 0, SCAN_DEV)
    device_of = jnp.arange(EDGES, dtype=jnp.int32) // EDGE_DEV
    region_of = device_of // N_PAIR
    low_side = jnp.where(region_of == 0, 1, 0)
    high_side = jnp.where(region_of == N_REGION - 1, 2, 3)
    side = low_side + jax.random.randint(second, (EDGES,), 0, 1 << 20) % (high_side - low_side)
    offset = jax.random.randint(third, (EDGES,), 0, SCAN_DEV)
    offset = jnp.where((side == 1) & (offset == own_scan), (offset + 1) % SCAN_DEV, offset)
    neighbor = side * SCAN_DEV + offset
    neighbor = neighbor.at[0].set(3 * SCAN_DEV - 1)
    neighbor = neighbor.at[(N_REGION * N_PAIR - 1) * EDGE_DEV].set(0)
    own_scan = own_scan.at[0].set(0)
    return (own_scan.astype(jnp.int32), neighbor.astype(jnp.int32))


def draw_edge_scan(key, part):
    return edge_helper(key)[0]


def draw_edge_nbr(key, part):
    return edge_helper(key)[1]


def draw_block_count(key, part):
    counts = jax.random.randint(jax.random.fold_in(key, 3), (BLOCKS,), 0, PTS + 1)
    return counts.at[0].set(PTS).astype(jnp.int32)


def place_ends(values, rng, least, high):
    shape = values.shape
    spot = [jax.random.randint(jax.random.fold_in(rng, axis), (), 0, shape[axis]) for axis in range(len(shape))]
    values = values.at[tuple(spot)].set(least)
    longest = shape.index(max(shape))
    spot[longest] = (spot[longest] + 1) % shape[longest]
    return values.at[tuple(spot)].set(high)


def block_scale(key, extent, cuts, smallest, largest):
    gain, own = 1.0, jax.random.fold_in(key, 6)
    for dim, parts in cuts:
        heights = jnp.exp(jax.random.uniform(jax.random.fold_in(own, dim), (parts,), jnp.float32, smallest / len(cuts), largest / len(cuts)))
        gain = gain * jnp.repeat(heights, extent[dim] // parts).reshape([-1 if axis == dim else 1 for axis in range(len(extent))])
    return gain


def bell_draw(stream_key, shape, deviation, limit, shards=(), held_as=jnp.bfloat16):
    factor_of = block_scale(stream_key, shape, shards, -0.22, 0.18) if shards else 1.0
    values = jax.random.normal(stream_key, shape, jnp.float32) * deviation * factor_of
    return jnp.minimum(jnp.maximum(values, -limit), limit).astype(held_as)


def setup_inputs(seed: int = 0) -> dict:
    key_list = jax.random.split(jax.random.key(seed), 9)
    points = bell_draw(key_list[0], (3, BLOCKS, PTS), 1.0, 6.0, ((1, 128),), jnp.float32)
    offsets = bell_draw(key_list[1], (3, BLOCKS, PTS), 2.0, 12.0, ((1, 128),), jnp.float32)
    normals = bell_draw(key_list[2], (3, BLOCKS, PTS), 1.0, 6.0, ((1, 128),), jnp.float32)
    block_count = draw_block_count(jax.random.fold_in(key_list[8], 71), 0)
    block_edge = place_ends(jax.random.randint(key_list[4], (BLOCKS,), 0, EDGE_DEV), jax.random.fold_in(key_list[4], 1), 0, EDGE_DEV - 1).astype(jnp.int32)
    edge_scan = draw_edge_scan(jax.random.fold_in(key_list[8], 71), 0)
    edge_nbr = draw_edge_nbr(jax.random.fold_in(key_list[8], 71), 0)
    rotvec = jnp.clip(jax.random.uniform(key_list[7], (3, SCANS), jnp.float32, -0.3, 0.3) * block_scale(key_list[7], (3, SCANS), ((1, 128),), -0.4, 0.0), -0.3, 0.3)
    return {"points": points, "offsets": offsets, "normals": normals, "block_count": block_count, "block_edge": block_edge, "edge_scan": edge_scan, "edge_nbr": edge_nbr, "rotvec": rotvec}


damping = 16.0
min_length = 0.1

def exp_rotation(vector):
    theta_sq = vector[0] * vector[0] + vector[1] * vector[1] + vector[2] * vector[2]
    first = 1.0 - theta_sq / 6.0 + theta_sq ** 2 / 120.0 - theta_sq ** 3 / 5040.0 + theta_sq ** 4 / 362880.0
    second = 0.5 - theta_sq / 24.0 + theta_sq ** 2 / 720.0 - theta_sq ** 3 / 40320.0 + theta_sq ** 4 / 3628800.0
    skew_rows = [[None, -vector[2], vector[1]], [vector[2], None, -vector[0]], [-vector[1], vector[0], None]]
    entries = []
    for row in range(3):
        for col in range(3):
            value = second * vector[row] * vector[col]
            if row == col:
                value = value + 1.0 - second * theta_sq
            else:
                value = value + first * skew_rows[row][col]
            entries.append(value)
    return jnp.stack(entries)

def log_rotation(matrix):
    cosine = (matrix[0] + matrix[4] + matrix[8] - 1.0) * 0.5
    axis_vec = 0.5 * jnp.stack([matrix[7] - matrix[5], matrix[2] - matrix[6], matrix[3] - matrix[1]])
    sine = jnp.sqrt(lax.optimization_barrier(jnp.sum(axis_vec * axis_vec, axis=0)))
    theta = jnp.arctan2(sine, cosine)
    factor = jnp.where(sine < 0.0001, 1.0 + sine * sine / 6.0, theta / jnp.maximum(sine, 0.0001))
    return factor * axis_vec

def mat_mul(left, right):
    return jnp.stack([sum((left[3 * a + b] * right[3 * b + c] for b in range(3))) for a in range(3) for c in range(3)])

def mat_tmul(left, right):
    return jnp.stack([sum((left[3 * b + a] * right[3 * b + c] for b in range(3))) for a in range(3) for c in range(3)])

def solve_six(matrix, rhs):
    lower = [[None] * 6 for _ in range(6)]
    for col in range(6):
        diag_val = matrix[col, col] - sum((lower[col][k] * lower[col][k] for k in range(col))) if col else matrix[col, col]
        lower[col][col] = jnp.sqrt(diag_val)
        for row in range(col + 1, 6):
            value = matrix[row, col] - sum((lower[row][k] * lower[col][k] for k in range(col))) if col else matrix[row, col]
            lower[row][col] = value / lower[col][col]
    inter = []
    for row in range(6):
        value = rhs[row] - sum((lower[row][k] * inter[k] for k in range(row))) if row else rhs[row]
        inter.append(value / lower[row][row])
    result = [None] * 6
    for row in range(5, -1, -1):
        value = inter[row] - sum((lower[k][row] * result[k] for k in range(row + 1, 6))) if row < 5 else inter[row]
        result[row] = value / lower[row][row]
    return jnp.stack(result)

def normal_terms(src_pts, offset, normal):
    cross = jnp.stack([src_pts[1] * normal[2] - src_pts[2] * normal[1], src_pts[2] * normal[0] - src_pts[0] * normal[2], src_pts[0] * normal[1] - src_pts[1] * normal[0]])
    jacobian = jnp.concatenate([cross, normal], axis=0)
    resid = lax.optimization_barrier(jnp.sum(normal * offset, axis=0))
    hess = jnp.einsum('ibw,jbw->ijb', jacobian, jacobian, precision=lax.Precision.HIGHEST)
    grad = jnp.einsum('ibw,bw->ib', jacobian, resid, precision=lax.Precision.HIGHEST)
    return jnp.concatenate([hess.reshape(36, -1), grad], axis=0)

def slot_table(block_edge, count):
    return (block_edge[:, None] == jnp.arange(count, dtype=jnp.int32)[None, :]).astype(jnp.float32)

def slot_sums(terms, block_edge, count):
    return jnp.dot(terms, slot_table(block_edge, count), precision=lax.Precision.HIGHEST)

def slot_live(filled, block_edge, count):
    hits = jnp.dot(filled[None, :], slot_table(block_edge, count), precision=lax.Precision.HIGHEST)[0]
    return (hits > 0.5).astype(jnp.float32)

def solve_poses(sums):
    hess = sums[:36].reshape(6, 6, -1) + damping * jnp.eye(6, dtype=jnp.float32)[:, :, None]
    return -solve_six(hess, sums[36:])

def reference(points, offsets, normals, block_count, block_edge, edge_scan, edge_nbr, rotvec):
    devices = N_REGION * N_PAIR

    def by_owner(array):
        return array.reshape(3, devices, devices, SLOT, PTS).transpose(2, 0, 1, 3, 4).reshape(devices, 3, devices * SLOT, PTS)

    def ints_by_owner(array):
        return array.reshape(devices, devices, SLOT).transpose(1, 0, 2).reshape(devices, devices * SLOT)

    def one_owner(items):
        src_pts, offset, normal, count, owner_edge = items
        width = jnp.arange(PTS, dtype=jnp.int32)
        block_mask = (width[None, :] < count[:, None]).astype(jnp.float32)[None]
        terms = normal_terms(src_pts * block_mask, offset * block_mask, normal * block_mask)
        filled = (count > 0).astype(jnp.float32)
        return (slot_sums(terms, owner_edge, EDGE_DEV), slot_live(filled, owner_edge, EDGE_DEV))
    sums, live_mask = lax.map(one_owner, (by_owner(points), by_owner(offsets), by_owner(normals), ints_by_owner(block_count), ints_by_owner(block_edge)))
    sums = sums.reshape(devices, 42, devices, PSLOT).transpose(1, 2, 0, 3).reshape(42, EDGES)
    live_mask = live_mask.reshape(devices, devices, PSLOT).transpose(1, 0, 2).reshape(EDGES)
    pose_out = solve_poses(sums)
    relative = exp_rotation(pose_out[:3])
    device_of = jnp.arange(EDGES, dtype=jnp.int32) // EDGE_DEV
    scan_glob = device_of * SCAN_DEV + edge_scan
    nbr_glob = (device_of + (edge_nbr // SCAN_DEV - 1) * N_PAIR) * SCAN_DEV + edge_nbr % SCAN_DEV
    rotation = exp_rotation(rotvec)
    for sweep in range(SWEEPS):
        near = jnp.take(rotation, nbr_glob, axis=1)
        mine = jnp.take(rotation, scan_glob, axis=1)
        tangent = log_rotation(mat_tmul(mine, mat_mul(near, relative)))
        length = jnp.sqrt(lax.optimization_barrier(jnp.sum(tangent * tangent, axis=0)))
        weight = live_mask / jnp.maximum(length, min_length)
        numer = jax.ops.segment_sum((weight * tangent).T, scan_glob, SCANS).T
        denom = jax.ops.segment_sum(weight, scan_glob, SCANS) + 1.0
        rotation = mat_mul(rotation, exp_rotation(numer / denom))
    return (pose_out, rotation)
```

```python
import jax
import jax.numpy as jnp
from jax import lax
from jax.experimental import pallas as pl
from jax.experimental.pallas import tpu as pltpu
from jax.sharding import PartitionSpec as P

DAMPING = 16.0
MIN_LENGTH = 0.1
LANES = 128
TILES = 8
AXES = ("region", "pair")
F32 = jnp.float32
BF16 = jnp.bfloat16

UPPER = [(a, b) for a in range(6) for b in range(a, 6)]
SLOT_OF = {pair: i for i, pair in enumerate(UPPER)}
N_TERMS = 27
ROW_FILL = 27
ROW_EDGE = 28


def three_parts(x):
    high = x.astype(BF16).astype(F32)
    rest = x - high
    mid = rest.astype(BF16).astype(F32)
    return jnp.concatenate([high, mid, rest - mid], axis=0).astype(BF16)


def add_parts(x):
    n = x.shape[0] // 3
    return x[:n] + x[n : 2 * n] + x[2 * n :]


def dot_nn(a, b):
    return lax.dot_general(a, b, (((1,), (0,)), ((), ())), preferred_element_type=F32)


def dot_nt(a, b):
    return lax.dot_general(a, b, (((1,), (1,)), ((), ())), preferred_element_type=F32)


def terms_kernel(cnt_ref, edge_ref, p_hbm, d_hbm, n_hbm, out_ref, pbuf, dbuf, nbuf, tr, acc_ref, t_ref, sems):
    copies = []
    for t in range(TILES):
        rows = pl.ds(t * LANES, LANES)
        for a, (src, dst) in enumerate(((p_hbm, pbuf), (d_hbm, dbuf), (n_hbm, nbuf))):
            copies.append(pltpu.make_async_copy(src.at[:, rows, :], dst.at[:, rows, :], sems.at[a, t]))
    for c in copies:
        c.start()
    sub = lax.broadcasted_iota(jnp.int32, (8, LANES), 0)
    acc_ref[...] = jnp.zeros_like(acc_ref)

    def tile(t, carry):
        rows = pl.ds(pl.multiple_of(t * LANES, LANES), LANES)
        for a, (src, dst) in enumerate(((p_hbm, pbuf), (d_hbm, dbuf), (n_hbm, nbuf))):
            pltpu.make_async_copy(src.at[:, rows, :], dst.at[:, rows, :], sems.at[a, t]).wait()
        for a, buf in enumerate((pbuf, dbuf, nbuf)):
            for c in range(3):
                tr[3 * a + c] = buf[c, rows, :].T
        cnt = cnt_ref[pl.ds(t, 1), :]
        acc = [None] * N_TERMS
        for r in range(LANES // 8):
            at = pl.ds(8 * r, 8)
            keep = (sub + 8 * r) < cnt
            p = [tr[c, at, :] for c in range(3)]
            d = [tr[3 + c, at, :] for c in range(3)]
            n = [jnp.where(keep, tr[6 + c, at, :], 0.0) for c in range(3)]
            jac = [p[1] * n[2] - p[2] * n[1], p[2] * n[0] - p[0] * n[2], p[0] * n[1] - p[1] * n[0]] + n
            resid = n[0] * d[0] + n[1] * d[1] + n[2] * d[2]
            prods = [jac[a] * jac[b] for a, b in UPPER] + [j * resid for j in jac]
            acc = [x if y is None else y + x for x, y in zip(prods, acc)]
        for c in range(N_TERMS):
            acc_ref[pl.ds(8 * c, 8), :] = acc[c]
        acc_ref[pl.ds(8 * ROW_FILL, 1), :] = (cnt > 0).astype(F32)
        acc_ref[pl.ds(8 * ROW_EDGE, 1), :] = edge_ref[pl.ds(t, 1), :].astype(F32)
        total = acc_ref[pl.ds(0, 32, stride=8), :]
        for r in range(1, 8):
            total = total + acc_ref[pl.ds(r, 32, stride=8), :]
        t_ref[...] = jnp.concatenate([total, jnp.zeros((96, LANES), F32)], axis=0).T
        for h in range(2):
            parts = [t_ref[pl.ds(4 * h + k, 16, stride=8), :][:, :32] for k in range(4)]
            out_ref[pl.ds(t * 32 + h, 16, stride=2), :] = jnp.concatenate(parts, axis=1)
        return carry

    lax.fori_loop(0, TILES, tile, 0)


def block_terms(points, offsets, normals, count, edge):
    any_spec = pl.BlockSpec(memory_space=pl.ANY)
    vmem = pl.BlockSpec(memory_space=pltpu.VMEM)
    return pl.pallas_call(
        terms_kernel,
        out_shape=jax.ShapeDtypeStruct((256, LANES), F32),
        in_specs=[vmem, vmem, any_spec, any_spec, any_spec],
        out_specs=vmem,
        scratch_shapes=[
            pltpu.VMEM((3, 1024, LANES), F32),
            pltpu.VMEM((3, 1024, LANES), F32),
            pltpu.VMEM((3, 1024, LANES), F32),
            pltpu.VMEM((9, LANES, LANES), F32),
            pltpu.VMEM((256, LANES), F32),
            pltpu.VMEM((LANES, LANES), F32),
            pltpu.SemaphoreType.DMA((3, TILES)),
        ],
        compiler_params=pltpu.CompilerParams(vmem_limit_bytes=24 * 1024 * 1024),
        cost_estimate=pl.CostEstimate(flops=9_000_000, bytes_accessed=5_000_000, transcendentals=0),
        name="block_terms",
    )(count, edge, points, offsets, normals)


def solve_six(hess, rhs):
    low = {}
    inv = []
    work = dict(hess)
    z = list(rhs)
    for c in range(6):
        inv.append(1.0 / work[c, c])
        for r in range(c + 1, 6):
            low[r, c] = work[c, r] * inv[c]
        for a in range(c + 1, 6):
            for b in range(a, 6):
                work[a, b] = work[a, b] - low[a, c] * work[c, b]
            z[a] = z[a] - low[a, c] * z[c]
    x = [None] * 6
    for r in range(5, -1, -1):
        v = z[r] * inv[r]
        for k in range(r + 1, 6):
            v = v - low[k, r] * x[k]
        x[r] = v
    return x


def solve_kernel(in_ref, out_ref, s_ref, q_ref):
    row = lax.broadcasted_iota(jnp.int32, (256, LANES), 0)
    wanted = ((row % LANES) * 2 + row // LANES).astype(F32)
    lhs, hot = [], []
    for h in range(2):
        got = in_ref[pl.ds(h, LANES, stride=2), :].T
        for k in range(4):
            part = got[32 * k : 32 * k + 32]
            lhs.append(part)
            hot.append((wanted == part[ROW_EDGE : ROW_EDGE + 1]).astype(F32).astype(BF16))
    lhs = three_parts(jnp.concatenate(lhs, axis=1))
    sums = add_parts(dot_nt(lhs, jnp.concatenate(hot, axis=1)))
    s_ref[pl.ds(0, 32), :] = sums[:, :LANES]
    s_ref[pl.ds(32, 32), :] = sums[:, LANES:]
    term = [s_ref[pl.ds(c, 2, stride=32), :] for c in range(ROW_FILL + 1)]
    hess = {}
    for (a, b), i in SLOT_OF.items():
        hess[a, b] = term[i] + DAMPING if a == b else term[i]
    x = solve_six(hess, term[21:27])
    q_ref[...] = jnp.zeros_like(q_ref)
    for c in range(6):
        q_ref[pl.ds(c, 2, stride=8), :] = -x[c]
    q_ref[pl.ds(6, 2, stride=8), :] = (term[ROW_FILL] > 0.5).astype(F32)
    rows = q_ref[...].T[:, :16]
    lower = jnp.concatenate([rows[112:], rows[:112]], axis=0)
    upper = jnp.concatenate([rows[16:], rows[:16]], axis=0)
    out_ref[...] = jnp.concatenate([lower, rows, upper, jnp.zeros((LANES, 80), F32)], axis=1)


def pair_solve(got):
    vmem = pl.BlockSpec(memory_space=pltpu.VMEM)
    return pl.pallas_call(
        solve_kernel,
        out_shape=jax.ShapeDtypeStruct((LANES, LANES), F32),
        in_specs=[vmem],
        out_specs=vmem,
        scratch_shapes=[pltpu.VMEM((256, LANES), F32), pltpu.VMEM((LANES, LANES), F32)],
        cost_estimate=pl.CostEstimate(flops=50_000_000, bytes_accessed=200_000, transcendentals=0),
        name="pair_solve",
    )(got)


def exp_rotation(v):
    t = v[0] * v[0] + v[1] * v[1] + v[2] * v[2]
    first = 1.0 + t * (-1.0 / 6.0 + t * (1.0 / 120.0 + t * (-1.0 / 5040.0 + t * (1.0 / 362880.0))))
    second = 0.5 + t * (-1.0 / 24.0 + t * (1.0 / 720.0 + t * (-1.0 / 40320.0 + t * (1.0 / 3628800.0))))
    skew = [[None, -v[2], v[1]], [v[2], None, -v[0]], [-v[1], v[0], None]]
    out = []
    for a in range(3):
        for b in range(3):
            value = second * v[a] * v[b]
            value = value + (1.0 - second * t) if a == b else value + first * skew[a][b]
            out.append(value)
    return out


def mat_mul(x, y):
    return [x[3 * a] * y[c] + x[3 * a + 1] * y[3 + c] + x[3 * a + 2] * y[6 + c] for a in range(3) for c in range(3)]


def mat_tmul(x, y):
    return [x[a] * y[c] + x[3 + a] * y[3 + c] + x[6 + a] * y[6 + c] for a in range(3) for c in range(3)]


def angle_of(sine, cosine):
    size = jnp.abs(cosine)
    big = jnp.maximum(sine, size)
    small = jnp.minimum(sine, size)
    shift = small > 0.4142135623730950 * big
    top = jnp.where(shift, small - big, small)
    bottom = jnp.where(shift, small + big, big)
    x = top / jnp.maximum(bottom, 1e-30)
    z = x * x
    poly = ((8.05374449538e-2 * z - 1.38776856032e-1) * z + 1.99777106478e-1) * z - 3.33329491539e-1
    y = poly * z * x + x
    y = jnp.where(shift, y + 0.7853981633974483, y)
    y = jnp.where(sine > size, 1.5707963267948966 - y, y)
    return jnp.where(cosine < 0.0, 3.141592653589793 - y, y)


def log_rotation(m):
    cosine = (m[0] + m[4] + m[8] - 1.0) * 0.5
    u = [0.5 * (m[7] - m[5]), 0.5 * (m[2] - m[6]), 0.5 * (m[3] - m[1])]
    sine_sq = u[0] * u[0] + u[1] * u[1] + u[2] * u[2]
    sine = jnp.sqrt(sine_sq)
    theta = angle_of(sine, cosine)
    factor = jnp.where(sine < 0.0001, 1.0 + sine_sq / 6.0, theta / jnp.maximum(sine, 0.0001))
    return [factor * u[0], factor * u[1], factor * u[2]]


def sweep_kernel(in_ref, v0, v1, v2, v3, v4, pose_ref, rot_ref, two_ref, s_ref, x_ref, e_ref, n_ref, m_ref, w_ref, d_ref):
    got = in_ref[...]
    two_ref[pl.ds(0, LANES, stride=2), :] = got
    two_ref[pl.ds(1, LANES, stride=2), :] = pltpu.roll(got, LANES - 8, 1)
    for h in range(2):
        part = two_ref[pl.ds(h * LANES, LANES), :].T
        for g in range(3):
            s_ref[pl.ds(16 * g + 8 * h, 8), :] = part[16 * g : 16 * g + 8]
        pose_ref[:, h * LANES : (h + 1) * LANES] = part[16:22]
    relative = exp_rotation([s_ref[pl.ds(c, 6, stride=8), :] for c in range(3)])
    live = s_ref[pl.ds(6, 6, stride=8), :]

    for i, v in enumerate((v0, v1, v2, v3, v4)):
        x_ref[pl.ds(8 * i, 8), :] = v[...]
    start = exp_rotation([x_ref[pl.ds(c, 5, stride=8), :] for c in range(3)])
    e_ref[...] = jnp.zeros_like(e_ref)
    for c in range(9):
        e_ref[pl.ds(c, 5, stride=16), :] = start[c]
    w_ref[...] = jnp.zeros_like(w_ref)

    scan = lax.broadcasted_iota(jnp.int32, (LANES, LANES), 0).astype(F32)
    near_scan = lax.broadcasted_iota(jnp.int32, (3 * LANES, LANES), 0).astype(F32)
    own_hot, near_hot = [], []
    for g in range(3):
        ids = x_ref[pl.ds(8 * (g + 1), 8), :]
        own_hot.append([(scan == ids[3 + h : 4 + h]).astype(F32).astype(BF16) for h in range(2)])
        near_hot.append([(near_scan == ids[5 + h : 6 + h]).astype(F32).astype(BF16) for h in range(2)])

    def sweep(parts, groups, relative, live, current):
        count = len(groups)
        for i, g in enumerate(groups):
            around = jnp.concatenate(parts[i : i + 3], axis=1)
            for h in range(2):
                at = pl.ds((2 * i + h) * 16, 16)
                n_ref[at, :] = add_parts(dot_nn(around, near_hot[g][h]))
                m_ref[at, :] = add_parts(dot_nn(parts[i + 1], own_hot[g][h]))
        near = [n_ref[pl.ds(c, 2 * count, stride=16), :] for c in range(9)]
        mine = [m_ref[pl.ds(c, 2 * count, stride=16), :] for c in range(9)]
        tangent = log_rotation(mat_tmul(mine, mat_mul(near, relative)))
        length = jnp.sqrt(tangent[0] * tangent[0] + tangent[1] * tangent[1] + tangent[2] * tangent[2])
        weight = live / jnp.maximum(length, MIN_LENGTH)
        for c in range(3):
            w_ref[pl.ds(c, 2 * count, stride=16), :] = weight * tangent[c]
        w_ref[pl.ds(3, 2 * count, stride=16), :] = weight
        for i, g in enumerate(groups):
            left = jnp.concatenate([w_ref[pl.ds((2 * i + h) * 16, 16), :] for h in range(2)], axis=1)
            total = add_parts(dot_nt(three_parts(left), jnp.concatenate(own_hot[g], axis=1)))
            d_ref[pl.ds(8 * i, 8), :] = total[:8]
        inv = 1.0 / (d_ref[pl.ds(3, count, stride=8), :] + 1.0)
        delta = [d_ref[pl.ds(c, count, stride=8), :] * inv for c in range(3)]
        return mat_mul(current, exp_rotation(delta))

    parts = [three_parts(e_ref[pl.ds(16 * i, 16), :]) for i in range(5)]
    current = [e_ref[pl.ds(16 + c, 3, stride=16), :] for c in range(9)]
    middle = sweep(parts, [0, 1, 2], relative, live, current)
    for c in range(9):
        e_ref[pl.ds(c, 3, stride=16), :] = middle[c]
    parts = [three_parts(e_ref[pl.ds(16 * i, 16), :]) for i in range(3)]
    final = sweep(parts, [1], [r[2:4] for r in relative], live[2:4], [m[1:2] for m in middle])
    for c in range(9):
        rot_ref[pl.ds(c, 1), :] = final[c]


def sweeps(got, packs):
    vmem = pl.BlockSpec(memory_space=pltpu.VMEM)
    return pl.pallas_call(
        sweep_kernel,
        out_shape=(jax.ShapeDtypeStruct((6, 256), F32), jax.ShapeDtypeStruct((9, LANES), F32)),
        in_specs=[vmem] * 6,
        out_specs=(vmem, vmem),
        scratch_shapes=[
            pltpu.VMEM((256, LANES), F32),
            pltpu.VMEM((64, LANES), F32),
            pltpu.VMEM((64, LANES), F32),
            pltpu.VMEM((144, LANES), F32),
            pltpu.VMEM((128, LANES), F32),
            pltpu.VMEM((128, LANES), F32),
            pltpu.VMEM((128, LANES), F32),
            pltpu.VMEM((64, LANES), F32),
        ],
        cost_estimate=pl.CostEstimate(flops=60_000_000, bytes_accessed=200_000, transcendentals=0),
        name="sweeps",
    )(got, *packs)


def on_device(points, offsets, normals, block_count, block_edge, edge_scan, edge_nbr, rotvec):
    terms = block_terms(points, offsets, normals, block_count.reshape(8, LANES), block_edge.reshape(8, LANES))
    own = jnp.concatenate(
        [
            rotvec,
            edge_scan.reshape(2, LANES).astype(F32),
            edge_nbr.reshape(2, LANES).astype(F32),
            jnp.zeros((1, LANES), F32),
        ],
        axis=0,
    )
    count = lax.axis_size("region")

    def from_region(step):
        return lax.ppermute(own, "region", [((i + step) % count, i) for i in range(count)])

    packs = [from_region(-2), from_region(-1), own, from_region(1), from_region(2)]
    moved = lax.all_to_all(terms, AXES, split_axis=0, concat_axis=0, tiled=True)
    solved = pair_solve(moved)
    returned = lax.all_to_all(solved, AXES, split_axis=0, concat_axis=0, tiled=True)
    return sweeps(returned, packs)


def solution(mesh):
    placed = (
        P(None, AXES, None),
        P(None, AXES, None),
        P(None, AXES, None),
        P(AXES),
        P(AXES),
        P(AXES),
        P(AXES),
        P(None, AXES),
    )
    return jax.shard_map(
        on_device,
        mesh=mesh,
        in_specs=placed,
        out_specs=(P(None, AXES), P(None, AXES)),
        check_vma=False,
    )
```

```python
import jax
import jax.numpy as jnp
from jax import lax
from jax.experimental import pallas as pl
from jax.experimental.pallas import tpu as pltpu
from jax.sharding import PartitionSpec as P

DAMPING = 16.0
MIN_LENGTH = 0.1
LANES = 128
TILES = 8
CHUNKS = 2
TILES_IN_CHUNK = TILES // CHUNKS
CHUNK = TILES_IN_CHUNK * LANES
AXES = ("region", "pair")
F32 = jnp.float32
BF16 = jnp.bfloat16

UPPER = [(a, b) for a in range(6) for b in range(a, 6)]
SLOT_OF = {pair: i for i, pair in enumerate(UPPER)}
N_TERMS = 27
ROW_FILL = 27
ROW_EDGE = 28


def three_parts(x):
    high = x.astype(BF16).astype(F32)
    rest = x - high
    mid = rest.astype(BF16).astype(F32)
    return jnp.concatenate([high, mid, rest - mid], axis=0).astype(BF16)


def add_parts(x):
    n = x.shape[0] // 3
    return x[:n] + x[n : 2 * n] + x[2 * n :]


def dot_nn(a, b):
    return lax.dot_general(a, b, (((1,), (0,)), ((), ())), preferred_element_type=F32)


def dot_nt(a, b):
    return lax.dot_general(a, b, (((1,), (1,)), ((), ())), preferred_element_type=F32)


def terms_kernel(cnt_hbm, edge_hbm, p_hbm, d_hbm, n_hbm, out_ref, cnt_ref, edge_ref, pbuf, dbuf, nbuf, tr, acc_ref, t_ref, sems, id_sems):
    def chunk_copies(i):
        rows = pl.ds(i * CHUNK, CHUNK)
        pairs = ((n_hbm, nbuf), (p_hbm, pbuf), (d_hbm, dbuf))
        return [pltpu.make_async_copy(src.at[:, rows, :], dst.at[:, rows, :], sems.at[a, i]) for a, (src, dst) in enumerate(pairs)]

    id_copies = [
        pltpu.make_async_copy(cnt_hbm, cnt_ref, id_sems.at[0]),
        pltpu.make_async_copy(edge_hbm, edge_ref, id_sems.at[1]),
    ]
    for i in range(CHUNKS):
        for c in chunk_copies(i):
            c.start()
        if i == 0:
            for c in id_copies:
                c.start()
    sub = lax.broadcasted_iota(jnp.int32, (8, LANES), 0)
    fourth = lax.broadcasted_iota(jnp.int32, (32, LANES), 1) % 4
    acc_ref[...] = jnp.zeros_like(acc_ref)
    for c in id_copies:
        c.wait()

    def send_rows(i):
        for u in range(TILES_IN_CHUNK):
            total = acc_ref[u, pl.ds(0, 32, stride=8), :]
            for r in range(1, 8):
                total = total + acc_ref[u, pl.ds(r, 32, stride=8), :]
            spread = jnp.concatenate([jnp.where(fourth == k, total, 0.0) for k in range(4)], axis=0)
            t_ref[u] = spread.T
        for u in range(TILES_IN_CHUNK):
            for h in range(2):
                rows = t_ref[u, pl.ds(4 * h, 16, stride=8), :]
                for k in range(1, 4):
                    rows = rows + t_ref[u, pl.ds(4 * h + k, 16, stride=8), :]
                out_ref[pl.ds((i * TILES_IN_CHUNK + u) * 32 + h, 16, stride=2), :] = rows

    def chunk(i, carry):
        for c in chunk_copies(i):
            c.wait()
        send_rows(jnp.maximum(i - 1, 0))
        for u in range(TILES_IN_CHUNK):
            t = i * TILES_IN_CHUNK + u
            rows = pl.ds(pl.multiple_of(t * LANES, LANES), LANES)
            for a, buf in enumerate((pbuf, dbuf, nbuf)):
                for c in range(3):
                    tr[u, 3 * a + c] = buf[c, rows, :].T
            cnt = cnt_ref[pl.ds(t, 1), :]
            acc = [None] * N_TERMS
            for r in range(LANES // 8):
                at = pl.ds(8 * r, 8)
                keep = (sub + 8 * r) < cnt
                p = [tr[u, c, at, :] for c in range(3)]
                d = [tr[u, 3 + c, at, :] for c in range(3)]
                n = [jnp.where(keep, tr[u, 6 + c, at, :], 0.0) for c in range(3)]
                jac = [p[1] * n[2] - p[2] * n[1], p[2] * n[0] - p[0] * n[2], p[0] * n[1] - p[1] * n[0]] + n
                resid = n[0] * d[0] + n[1] * d[1] + n[2] * d[2]
                prods = [jac[a] * jac[b] for a, b in UPPER] + [j * resid for j in jac]
                acc = [x if y is None else y + x for x, y in zip(prods, acc)]
            for c in range(N_TERMS):
                acc_ref[u, pl.ds(8 * c, 8), :] = acc[c]
            acc_ref[u, pl.ds(8 * ROW_FILL, 1), :] = (cnt > 0).astype(F32)
            acc_ref[u, pl.ds(8 * ROW_EDGE, 1), :] = edge_ref[pl.ds(t, 1), :].astype(F32)
        return carry

    lax.fori_loop(0, CHUNKS, chunk, 0)
    send_rows(CHUNKS - 1)


def block_terms(points, offsets, normals, count, edge):
    hbm = pl.BlockSpec(memory_space=pl.ANY)
    vmem = pl.BlockSpec(memory_space=pltpu.VMEM)
    return pl.pallas_call(
        terms_kernel,
        out_shape=jax.ShapeDtypeStruct((256, LANES), F32),
        in_specs=[hbm] * 5,
        out_specs=vmem,
        scratch_shapes=[
            pltpu.VMEM((8, LANES), jnp.int32),
            pltpu.VMEM((8, LANES), jnp.int32),
            pltpu.VMEM((3, 1024, LANES), F32),
            pltpu.VMEM((3, 1024, LANES), F32),
            pltpu.VMEM((3, 1024, LANES), F32),
            pltpu.VMEM((TILES_IN_CHUNK, 9, LANES, LANES), F32),
            pltpu.VMEM((TILES_IN_CHUNK, 256, LANES), F32),
            pltpu.VMEM((TILES_IN_CHUNK, LANES, LANES), F32),
            pltpu.SemaphoreType.DMA((3, CHUNKS)),
            pltpu.SemaphoreType.DMA((2,)),
        ],
        compiler_params=pltpu.CompilerParams(vmem_limit_bytes=60 * 1024 * 1024),
        cost_estimate=pl.CostEstimate(flops=9_000_000, bytes_accessed=5_000_000, transcendentals=0),
        name="block_terms",
    )(count, edge, points, offsets, normals)


def solve_six(hess, rhs):
    low = {}
    inv = []
    work = dict(hess)
    z = list(rhs)
    for c in range(6):
        inv.append(1.0 / work[c, c])
        for r in range(c + 1, 6):
            low[r, c] = work[c, r] * inv[c]
        for a in range(c + 1, 6):
            for b in range(a, 6):
                work[a, b] = work[a, b] - low[a, c] * work[c, b]
            z[a] = z[a] - low[a, c] * z[c]
    x = [None] * 6
    for r in range(5, -1, -1):
        v = z[r] * inv[r]
        for k in range(r + 1, 6):
            v = v - low[k, r] * x[k]
        x[r] = v
    return x


def solve_kernel(in_ref, out_ref, s_ref, q_ref):
    row = lax.broadcasted_iota(jnp.int32, (256, LANES), 0)
    wanted = ((row % LANES) * 2 + row // LANES).astype(F32)
    lhs, hot = [], []
    for h in range(2):
        got = in_ref[pl.ds(h, LANES, stride=2), :].T
        for k in range(4):
            part = got[32 * k : 32 * k + 32]
            lhs.append(part)
            hot.append((wanted == part[ROW_EDGE : ROW_EDGE + 1]).astype(F32).astype(BF16))
    lhs = three_parts(jnp.concatenate(lhs, axis=1))
    sums = add_parts(dot_nt(lhs, jnp.concatenate(hot, axis=1)))
    s_ref[pl.ds(0, 32), :] = sums[:, :LANES]
    s_ref[pl.ds(32, 32), :] = sums[:, LANES:]
    term = [s_ref[pl.ds(c, 2, stride=32), :] for c in range(ROW_FILL + 1)]
    hess = {}
    for (a, b), i in SLOT_OF.items():
        hess[a, b] = term[i] + DAMPING if a == b else term[i]
    x = solve_six(hess, term[21:27])
    q_ref[...] = jnp.zeros_like(q_ref)
    for c in range(6):
        q_ref[pl.ds(c, 2, stride=8), :] = -x[c]
    q_ref[pl.ds(6, 2, stride=8), :] = (term[ROW_FILL] > 0.5).astype(F32)
    rows = q_ref[...].T[:, :16]
    lower = jnp.concatenate([rows[112:], rows[:112]], axis=0)
    upper = jnp.concatenate([rows[16:], rows[:16]], axis=0)
    out_ref[...] = jnp.concatenate([lower, rows, upper, jnp.zeros((LANES, 80), F32)], axis=1)


def pair_solve(got):
    vmem = pl.BlockSpec(memory_space=pltpu.VMEM)
    return pl.pallas_call(
        solve_kernel,
        out_shape=jax.ShapeDtypeStruct((LANES, LANES), F32),
        in_specs=[vmem],
        out_specs=vmem,
        scratch_shapes=[pltpu.VMEM((256, LANES), F32), pltpu.VMEM((LANES, LANES), F32)],
        compiler_params=pltpu.CompilerParams(vmem_limit_bytes=8 * 1024 * 1024),
        cost_estimate=pl.CostEstimate(flops=50_000_000, bytes_accessed=200_000, transcendentals=0),
        name="pair_solve",
    )(got)


def exp_rotation(v):
    t = v[0] * v[0] + v[1] * v[1] + v[2] * v[2]
    first = 1.0 + t * (-1.0 / 6.0 + t * (1.0 / 120.0 + t * (-1.0 / 5040.0 + t * (1.0 / 362880.0))))
    second = 0.5 + t * (-1.0 / 24.0 + t * (1.0 / 720.0 + t * (-1.0 / 40320.0 + t * (1.0 / 3628800.0))))
    skew = [[None, -v[2], v[1]], [v[2], None, -v[0]], [-v[1], v[0], None]]
    out = []
    for a in range(3):
        for b in range(3):
            value = second * v[a] * v[b]
            value = value + (1.0 - second * t) if a == b else value + first * skew[a][b]
            out.append(value)
    return out


def mat_mul(x, y):
    return [x[3 * a] * y[c] + x[3 * a + 1] * y[3 + c] + x[3 * a + 2] * y[6 + c] for a in range(3) for c in range(3)]


def mat_tmul(x, y):
    return [x[a] * y[c] + x[3 + a] * y[3 + c] + x[6 + a] * y[6 + c] for a in range(3) for c in range(3)]


def angle_of(sine, cosine):
    size = jnp.abs(cosine)
    big = jnp.maximum(sine, size)
    small = jnp.minimum(sine, size)
    shift = small > 0.4142135623730950 * big
    top = jnp.where(shift, small - big, small)
    bottom = jnp.where(shift, small + big, big)
    x = top / jnp.maximum(bottom, 1e-30)
    z = x * x
    poly = ((8.05374449538e-2 * z - 1.38776856032e-1) * z + 1.99777106478e-1) * z - 3.33329491539e-1
    y = poly * z * x + x
    y = jnp.where(shift, y + 0.7853981633974483, y)
    y = jnp.where(sine > size, 1.5707963267948966 - y, y)
    return jnp.where(cosine < 0.0, 3.141592653589793 - y, y)


def log_rotation(m):
    cosine = (m[0] + m[4] + m[8] - 1.0) * 0.5
    u = [0.5 * (m[7] - m[5]), 0.5 * (m[2] - m[6]), 0.5 * (m[3] - m[1])]
    sine_sq = u[0] * u[0] + u[1] * u[1] + u[2] * u[2]
    sine = jnp.sqrt(sine_sq)
    theta = angle_of(sine, cosine)
    factor = jnp.where(sine < 0.0001, 1.0 + sine_sq / 6.0, theta / jnp.maximum(sine, 0.0001))
    return [factor * u[0], factor * u[1], factor * u[2]]


def sweep_kernel(in_ref, v0, v1, v2, v3, v4, pose_ref, rot_ref, two_ref, s_ref, x_ref, e_ref, n_ref, m_ref, w_ref, d_ref):
    got = in_ref[...]
    two_ref[pl.ds(0, LANES, stride=2), :] = got
    two_ref[pl.ds(1, LANES, stride=2), :] = pltpu.roll(got, LANES - 8, 1)
    for h in range(2):
        part = two_ref[pl.ds(h * LANES, LANES), :].T
        for g in range(3):
            s_ref[pl.ds(16 * g + 8 * h, 8), :] = part[16 * g : 16 * g + 8]
        pose_ref[:, h * LANES : (h + 1) * LANES] = part[16:22]
    relative = exp_rotation([s_ref[pl.ds(c, 6, stride=8), :] for c in range(3)])
    live = s_ref[pl.ds(6, 6, stride=8), :]

    for i, v in enumerate((v0, v1, v2, v3, v4)):
        x_ref[pl.ds(8 * i, 8), :] = v[...]
    start = exp_rotation([x_ref[pl.ds(c, 5, stride=8), :] for c in range(3)])
    e_ref[...] = jnp.zeros_like(e_ref)
    for c in range(9):
        e_ref[pl.ds(c, 5, stride=16), :] = start[c]
    w_ref[...] = jnp.zeros_like(w_ref)

    scan = lax.broadcasted_iota(jnp.int32, (LANES, LANES), 0).astype(F32)
    near_scan = lax.broadcasted_iota(jnp.int32, (3 * LANES, LANES), 0).astype(F32)
    own_hot, near_hot = [], []
    for g in range(3):
        ids = x_ref[pl.ds(8 * (g + 1), 8), :]
        own_hot.append([(scan == ids[3 + h : 4 + h]).astype(F32).astype(BF16) for h in range(2)])
        near_hot.append([(near_scan == ids[5 + h : 6 + h]).astype(F32).astype(BF16) for h in range(2)])

    def sweep(parts, groups, relative, live, current):
        count = len(groups)
        for i, g in enumerate(groups):
            around = jnp.concatenate(parts[i : i + 3], axis=1)
            for h in range(2):
                at = pl.ds((2 * i + h) * 16, 16)
                n_ref[at, :] = add_parts(dot_nn(around, near_hot[g][h]))
                m_ref[at, :] = add_parts(dot_nn(parts[i + 1], own_hot[g][h]))
        near = [n_ref[pl.ds(c, 2 * count, stride=16), :] for c in range(9)]
        mine = [m_ref[pl.ds(c, 2 * count, stride=16), :] for c in range(9)]
        tangent = log_rotation(mat_tmul(mine, mat_mul(near, relative)))
        length = jnp.sqrt(tangent[0] * tangent[0] + tangent[1] * tangent[1] + tangent[2] * tangent[2])
        weight = live / jnp.maximum(length, MIN_LENGTH)
        for c in range(3):
            w_ref[pl.ds(c, 2 * count, stride=16), :] = weight * tangent[c]
        w_ref[pl.ds(3, 2 * count, stride=16), :] = weight
        for i, g in enumerate(groups):
            left = jnp.concatenate([w_ref[pl.ds((2 * i + h) * 16, 16), :] for h in range(2)], axis=1)
            total = add_parts(dot_nt(three_parts(left), jnp.concatenate(own_hot[g], axis=1)))
            d_ref[pl.ds(8 * i, 8), :] = total[:8]
        inv = 1.0 / (d_ref[pl.ds(3, count, stride=8), :] + 1.0)
        delta = [d_ref[pl.ds(c, count, stride=8), :] * inv for c in range(3)]
        return mat_mul(current, exp_rotation(delta))

    parts = [three_parts(e_ref[pl.ds(16 * i, 16), :]) for i in range(5)]
    current = [e_ref[pl.ds(16 + c, 3, stride=16), :] for c in range(9)]
    middle = sweep(parts, [0, 1, 2], relative, live, current)
    for c in range(9):
        e_ref[pl.ds(c, 3, stride=16), :] = middle[c]
    parts = [three_parts(e_ref[pl.ds(16 * i, 16), :]) for i in range(3)]
    final = sweep(parts, [1], [r[2:4] for r in relative], live[2:4], [m[1:2] for m in middle])
    for c in range(9):
        rot_ref[pl.ds(c, 1), :] = final[c]


def sweeps(got, packs):
    vmem = pl.BlockSpec(memory_space=pltpu.VMEM)
    return pl.pallas_call(
        sweep_kernel,
        out_shape=(jax.ShapeDtypeStruct((6, 256), F32), jax.ShapeDtypeStruct((9, LANES), F32)),
        in_specs=[vmem] * 6,
        out_specs=(vmem, vmem),
        scratch_shapes=[
            pltpu.VMEM((256, LANES), F32),
            pltpu.VMEM((64, LANES), F32),
            pltpu.VMEM((64, LANES), F32),
            pltpu.VMEM((144, LANES), F32),
            pltpu.VMEM((128, LANES), F32),
            pltpu.VMEM((128, LANES), F32),
            pltpu.VMEM((128, LANES), F32),
            pltpu.VMEM((64, LANES), F32),
        ],
        compiler_params=pltpu.CompilerParams(vmem_limit_bytes=8 * 1024 * 1024),
        cost_estimate=pl.CostEstimate(flops=60_000_000, bytes_accessed=200_000, transcendentals=0),
        name="sweeps",
    )(got, *packs)


def on_device(points, offsets, normals, block_count, block_edge, edge_scan, edge_nbr, rotvec):
    terms = block_terms(points, offsets, normals, block_count.reshape(8, LANES), block_edge.reshape(8, LANES))
    own = jnp.concatenate(
        [
            rotvec,
            edge_scan.reshape(2, LANES).astype(F32),
            edge_nbr.reshape(2, LANES).astype(F32),
            jnp.zeros((1, LANES), F32),
        ],
        axis=0,
    )
    count = lax.axis_size("region")

    def from_region(step):
        return lax.ppermute(own, "region", [((i + step) % count, i) for i in range(count)])

    packs = [from_region(-2), from_region(-1), own, from_region(1), from_region(2)]
    moved = lax.all_to_all(terms, AXES, split_axis=0, concat_axis=0, tiled=True)
    solved = pair_solve(moved)
    returned = lax.all_to_all(solved, AXES, split_axis=0, concat_axis=0, tiled=True)
    return sweeps(returned, packs)


def solution(mesh):
    placed = (
        P(None, AXES, None),
        P(None, AXES, None),
        P(None, AXES, None),
        P(AXES),
        P(AXES),
        P(AXES),
        P(AXES),
        P(None, AXES),
    )
    return jax.shard_map(
        on_device,
        mesh=mesh,
        in_specs=placed,
        out_specs=(P(None, AXES), P(None, AXES)),
        check_vma=False,
    )
```

```python
import jax
import jax.numpy as jnp
from jax import lax
from jax.experimental import pallas as pl
from jax.experimental.pallas import tpu as pltpu
from jax.sharding import PartitionSpec as P

DAMPING = 16.0
MIN_LENGTH = 0.1
LANES = 128
TILES = 8
CHUNK_TILES = (4, 4)
AXES = ("region", "pair")
F32 = jnp.float32
BF16 = jnp.bfloat16

UPPER = [(a, b) for a in range(6) for b in range(a, 6)]
SLOT_OF = {pair: i for i, pair in enumerate(UPPER)}
N_TERMS = 27
ROW_FILL = 27
ROW_EDGE = 28
PACK_LANES = (29, 30, 31, 61, 62, 63, 93)
GROUP = 24
STEPS = (-32, -16, 0, 16, 32)


def three_parts(x):
    high = x.astype(BF16).astype(F32)
    rest = x - high
    mid = rest.astype(BF16).astype(F32)
    return jnp.concatenate([high, mid, rest - mid], axis=0).astype(BF16)


def add_parts(x):
    n = x.shape[0] // 3
    return x[:n] + x[n : 2 * n] + x[2 * n :]


def dot_nn(a, b):
    return lax.dot_general(a, b, (((1,), (0,)), ((), ())), preferred_element_type=F32)


def dot_nt(a, b):
    return lax.dot_general(a, b, (((1,), (1,)), ((), ())), preferred_element_type=F32)


def terms_kernel(cnt_hbm, edge_hbm, scan_hbm, nbr_hbm, vec_hbm, p_hbm, d_hbm, n_hbm, out_ref, cnt_ref, edge_ref, scan_ref, nbr_ref, vec_ref, pack_ref, pbuf, dbuf, nbuf, sum_ref, t_ref, sems, id_sems, *tr_refs):
    def chunk_copies(i):
        rows = pl.ds(sum(CHUNK_TILES[:i]) * LANES, CHUNK_TILES[i] * LANES)
        pairs = ((p_hbm, pbuf), (d_hbm, dbuf), (n_hbm, nbuf))
        return [pltpu.make_async_copy(src.at[:, rows, :], dst.at[:, rows, :], sems.at[a, i]) for a, (src, dst) in enumerate(pairs)]

    small = ((cnt_hbm, cnt_ref), (edge_hbm, edge_ref), (scan_hbm, scan_ref), (nbr_hbm, nbr_ref), (vec_hbm, vec_ref))
    id_copies = [pltpu.make_async_copy(src, dst, id_sems.at[i]) for i, (src, dst) in enumerate(small)]
    for i in range(len(CHUNK_TILES)):
        for c in chunk_copies(i):
            c.start()
        if i == 0:
            for c in id_copies:
                c.start()
    sub = lax.broadcasted_iota(jnp.int32, (8, LANES), 0)
    fourth = lax.broadcasted_iota(jnp.int32, (32, LANES), 1) % 4
    pack_ref[...] = jnp.zeros_like(pack_ref)
    for c in id_copies:
        c.wait()
    pack = [vec_ref[pl.ds(c, 1), :] for c in range(3)]
    pack += [ids[pl.ds(h, 1), :].astype(F32) for ids in (scan_ref, nbr_ref) for h in range(2)]
    for lane, row in zip(PACK_LANES, pack):
        pack_ref[pl.ds(lane, 1), :] = row
    pack_ref[...] = pack_ref[...].T

    def turn(t, tr):
        for a, buf in enumerate((pbuf, dbuf, nbuf)):
            for c in range(3):
                tr[3 * a + c] = buf[c, pl.ds(t * LANES, LANES), :].T

    def products(t, tr):
        cnt = cnt_ref[pl.ds(t, 1), :]
        acc = [None] * N_TERMS
        for r in range(LANES // 8):
            at = pl.ds(8 * r, 8)
            keep = (sub + 8 * r) < cnt
            p = [tr[c, at, :] for c in range(3)]
            n = [jnp.where(keep, tr[6 + c, at, :], 0.0) for c in range(3)]
            jac = [p[1] * n[2] - p[2] * n[1], p[2] * n[0] - p[0] * n[2], p[0] * n[1] - p[1] * n[0]] + n
            resid = n[0] * tr[3, at, :] + n[1] * tr[4, at, :] + n[2] * tr[5, at, :]
            prods = [jac[a] * jac[b] for a, b in UPPER] + [j * resid for j in jac]
            acc = [x if y is None else y + x for x, y in zip(prods, acc)]
        groups = [fold(fold_halves(acc[8 * g : 8 * g + 8]), 2) for g in range(3)]
        blank = jnp.zeros((8, LANES), F32)
        last = fold(fold_halves(acc[24:27] + [blank] * 5), 2)
        fill = jnp.broadcast_to((cnt > 0).astype(F32), (8, LANES))
        edge = jnp.broadcast_to(edge_ref[pl.ds(t, 1), :].astype(F32), (8, LANES))
        last = jnp.where(sub == ROW_FILL - 24, fill, jnp.where(sub == ROW_EDGE - 24, edge, last))
        sum_ref[pl.ds(32 * t, 32), :] = jnp.concatenate(groups + [last], axis=0)

    def fold_halves(v):
        out = []
        for x, y in zip(v[:4], v[4:]):
            out.append(jnp.where(sub < 4, x, y) + pltpu.roll(jnp.where(sub < 4, y, x), 4, 0))
        return out

    def fold(v, step):
        while step:
            low = sub % (2 * step) < step
            half = len(v) // 2
            v = [
                jnp.where(low, x + pltpu.roll(x, 8 - step, 0), y + pltpu.roll(y, step, 0))
                for x, y in zip(v[:half], v[half:])
            ]
            step //= 2
        return v[0]

    def spread(t):
        value = sum_ref[pl.ds(32 * t, 32), :]
        t_ref[t] = jnp.concatenate([jnp.where(fourth == k, value, 0.0) for k in range(4)], axis=0).T

    def send_rows(t):
        for q in range(4):
            value = fold([t_ref[t, pl.ds(32 * q + 8 * o, 8), :] for o in range(4)], 2)
            extra = pack_ref[pl.ds(16 * t + 4 * q, 4), :]
            out_ref[pl.ds(t * 32 + 8 * q, 4, stride=2), :] = value[:4] + extra
            out_ref[pl.ds(t * 32 + 8 * q + 1, 4, stride=2), :] = value[4:]

    def wait_chunk(i):
        for c in chunk_copies(i):
            c.wait()

    for i, tiles in enumerate(CHUNK_TILES):
        wait_chunk(i)
        for t in range(sum(CHUNK_TILES[:i]), sum(CHUNK_TILES[: i + 1])):
            tr = tr_refs[t % len(tr_refs)]
            turn(t, tr)
            products(t, tr)
    for t in range(TILES):
        spread(t)
    for t in range(TILES):
        send_rows(t)


def block_terms(points, offsets, normals, count, edge, scan, nbr, rotvec):
    hbm = pl.BlockSpec(memory_space=pl.ANY)
    vmem = pl.BlockSpec(memory_space=pltpu.VMEM)
    return pl.pallas_call(
        terms_kernel,
        out_shape=jax.ShapeDtypeStruct((256, LANES), F32),
        in_specs=[hbm] * 8,
        out_specs=vmem,
        scratch_shapes=[
            pltpu.VMEM((8, LANES), jnp.int32),
            pltpu.VMEM((8, LANES), jnp.int32),
            pltpu.VMEM((2, LANES), jnp.int32),
            pltpu.VMEM((2, LANES), jnp.int32),
            pltpu.VMEM((3, LANES), F32),
            pltpu.VMEM((LANES, LANES), F32),
            pltpu.VMEM((3, 1024, LANES), F32),
            pltpu.VMEM((3, 1024, LANES), F32),
            pltpu.VMEM((3, 1024, LANES), F32),
            pltpu.VMEM((32 * TILES, LANES), F32),
            pltpu.VMEM((TILES, LANES, LANES), F32),
            pltpu.SemaphoreType.DMA((3, len(CHUNK_TILES))),
            pltpu.SemaphoreType.DMA((5,)),
        ]
        + [pltpu.VMEM((9, LANES, LANES), F32)] * 4,
        compiler_params=pltpu.CompilerParams(vmem_limit_bytes=60 * 1024 * 1024),
        cost_estimate=pl.CostEstimate(flops=9_000_000, bytes_accessed=5_000_000, transcendentals=0),
        name="block_terms",
    )(count, edge, scan, nbr, rotvec, points, offsets, normals)


def solve_six(hess, rhs):
    low = {}
    inv = []
    work = dict(hess)
    z = list(rhs)
    for c in range(6):
        inv.append(1.0 / work[c, c])
        for r in range(c + 1, 6):
            low[r, c] = work[c, r] * inv[c]
        for a in range(c + 1, 6):
            for b in range(a, 6):
                work[a, b] = work[a, b] - low[a, c] * work[c, b]
            z[a] = z[a] - low[a, c] * z[c]
    x = [None] * 6
    for r in range(5, -1, -1):
        v = z[r] * inv[r]
        for k in range(r + 1, 6):
            v = v - low[k, r] * x[k]
        x[r] = v
    return x


def solve_kernel(in_ref, out_ref, s_ref, q_ref):
    row = lax.broadcasted_iota(jnp.int32, (256, LANES), 0)
    wanted = ((row % LANES) * 2 + row // LANES).astype(F32)
    lhs, hot = [], []
    for h in range(2):
        got = in_ref[pl.ds(h, LANES, stride=2), :].T
        if h == 0:
            pack = [got[lane : lane + 1] for lane in PACK_LANES]
        for k in range(4):
            part = got[32 * k : 32 * k + 32]
            lhs.append(part)
            hot.append((wanted == part[ROW_EDGE : ROW_EDGE + 1]).astype(F32).astype(BF16))
    lhs = three_parts(jnp.concatenate(lhs, axis=1))
    sums = add_parts(dot_nt(lhs, jnp.concatenate(hot, axis=1)))
    s_ref[pl.ds(0, 32), :] = sums[:, :LANES]
    s_ref[pl.ds(32, 32), :] = sums[:, LANES:]
    term = [s_ref[pl.ds(c, 2, stride=32), :] for c in range(ROW_FILL + 1)]
    hess = {}
    for (a, b), i in SLOT_OF.items():
        hess[a, b] = term[i] + DAMPING if a == b else term[i]
    x = solve_six(hess, term[21:27])
    middle = GROUP * 2
    q_ref[...] = jnp.zeros_like(q_ref)
    for c in range(6):
        q_ref[pl.ds(middle + c, 2, stride=8), :] = -x[c]
    q_ref[pl.ds(middle + 6, 2, stride=8), :] = (term[ROW_FILL] > 0.5).astype(F32)
    for r, row in enumerate(pack):
        q_ref[pl.ds(middle + 16 + r, 1), :] = row
    own = q_ref[pl.ds(middle, GROUP), :]
    for g, step in enumerate(STEPS):
        if step:
            q_ref[pl.ds(GROUP * g, GROUP), :] = pltpu.roll(own, -step % LANES, 1)
    out_ref[...] = q_ref[...].T


def pair_solve(got):
    vmem = pl.BlockSpec(memory_space=pltpu.VMEM)
    return pl.pallas_call(
        solve_kernel,
        out_shape=jax.ShapeDtypeStruct((LANES, LANES), F32),
        in_specs=[vmem],
        out_specs=vmem,
        scratch_shapes=[pltpu.VMEM((256, LANES), F32), pltpu.VMEM((LANES, LANES), F32)],
        compiler_params=pltpu.CompilerParams(vmem_limit_bytes=8 * 1024 * 1024),
        cost_estimate=pl.CostEstimate(flops=50_000_000, bytes_accessed=200_000, transcendentals=0),
        name="pair_solve",
    )(got)


def exp_rotation(v):
    t = v[0] * v[0] + v[1] * v[1] + v[2] * v[2]
    first = 1.0 + t * (-1.0 / 6.0 + t * (1.0 / 120.0 + t * (-1.0 / 5040.0 + t * (1.0 / 362880.0))))
    second = 0.5 + t * (-1.0 / 24.0 + t * (1.0 / 720.0 + t * (-1.0 / 40320.0 + t * (1.0 / 3628800.0))))
    skew = [[None, -v[2], v[1]], [v[2], None, -v[0]], [-v[1], v[0], None]]
    out = []
    for a in range(3):
        for b in range(3):
            value = second * v[a] * v[b]
            value = value + (1.0 - second * t) if a == b else value + first * skew[a][b]
            out.append(value)
    return out


def mat_mul(x, y):
    return [x[3 * a] * y[c] + x[3 * a + 1] * y[3 + c] + x[3 * a + 2] * y[6 + c] for a in range(3) for c in range(3)]


def mat_tmul(x, y):
    return [x[a] * y[c] + x[3 + a] * y[3 + c] + x[6 + a] * y[6 + c] for a in range(3) for c in range(3)]


def angle_of(sine, cosine):
    size = jnp.abs(cosine)
    big = jnp.maximum(sine, size)
    small = jnp.minimum(sine, size)
    shift = small > 0.4142135623730950 * big
    top = jnp.where(shift, small - big, small)
    bottom = jnp.where(shift, small + big, big)
    x = top / jnp.maximum(bottom, 1e-30)
    z = x * x
    poly = ((8.05374449538e-2 * z - 1.38776856032e-1) * z + 1.99777106478e-1) * z - 3.33329491539e-1
    y = poly * z * x + x
    y = jnp.where(shift, y + 0.7853981633974483, y)
    y = jnp.where(sine > size, 1.5707963267948966 - y, y)
    return jnp.where(cosine < 0.0, 3.141592653589793 - y, y)


def log_rotation(m):
    cosine = (m[0] + m[4] + m[8] - 1.0) * 0.5
    u = [0.5 * (m[7] - m[5]), 0.5 * (m[2] - m[6]), 0.5 * (m[3] - m[1])]
    sine_sq = u[0] * u[0] + u[1] * u[1] + u[2] * u[2]
    sine = jnp.sqrt(sine_sq)
    theta = angle_of(sine, cosine)
    factor = jnp.where(sine < 0.0001, 1.0 + sine_sq / 6.0, theta / jnp.maximum(sine, 0.0001))
    return [factor * u[0], factor * u[1], factor * u[2]]


def sweep_kernel(in_ref, pose_ref, rot_ref, two_ref, s_ref, x_ref, e_ref, n_ref, m_ref, w_ref, d_ref):
    got = in_ref[...]
    two_ref[pl.ds(0, LANES, stride=2), :] = got
    two_ref[pl.ds(1, LANES, stride=2), :] = pltpu.roll(got, LANES - 8, 1)
    for h in range(2):
        part = two_ref[pl.ds(h * LANES, LANES), :].T
        for g in range(3):
            first = GROUP * (g + 1)
            s_ref[pl.ds(16 * g + 8 * h, 8), :] = part[first : first + 8]
        pose_ref[:, h * LANES : (h + 1) * LANES] = part[2 * GROUP : 2 * GROUP + 6]
    relative = exp_rotation([s_ref[pl.ds(c, 6, stride=8), :] for c in range(3)])
    live = s_ref[pl.ds(6, 6, stride=8), :]

    packs = got.T
    for i in range(5):
        x_ref[pl.ds(8 * i, 8), :] = packs[GROUP * i + 16 : GROUP * i + 24]
    start = exp_rotation([x_ref[pl.ds(c, 5, stride=8), :] for c in range(3)])
    e_ref[...] = jnp.zeros_like(e_ref)
    for c in range(9):
        e_ref[pl.ds(c, 5, stride=16), :] = start[c]
    w_ref[...] = jnp.zeros_like(w_ref)

    scan = lax.broadcasted_iota(jnp.int32, (LANES, LANES), 0).astype(F32)
    near_scan = lax.broadcasted_iota(jnp.int32, (3 * LANES, LANES), 0).astype(F32)
    own_hot, near_hot = [], []
    for g in range(3):
        ids = x_ref[pl.ds(8 * (g + 1), 8), :]
        own_hot.append([(scan == ids[3 + h : 4 + h]).astype(F32).astype(BF16) for h in range(2)])
        near_hot.append([(near_scan == ids[5 + h : 6 + h]).astype(F32).astype(BF16) for h in range(2)])

    def sweep(parts, groups, relative, live, current):
        count = len(groups)
        for i, g in enumerate(groups):
            around = jnp.concatenate(parts[i : i + 3], axis=1)
            for h in range(2):
                at = pl.ds((2 * i + h) * 16, 16)
                n_ref[at, :] = add_parts(dot_nn(around, near_hot[g][h]))
                m_ref[at, :] = add_parts(dot_nn(parts[i + 1], own_hot[g][h]))
        near = [n_ref[pl.ds(c, 2 * count, stride=16), :] for c in range(9)]
        mine = [m_ref[pl.ds(c, 2 * count, stride=16), :] for c in range(9)]
        tangent = log_rotation(mat_tmul(mine, mat_mul(near, relative)))
        length = jnp.sqrt(tangent[0] * tangent[0] + tangent[1] * tangent[1] + tangent[2] * tangent[2])
        weight = live / jnp.maximum(length, MIN_LENGTH)
        for c in range(3):
            w_ref[pl.ds(c, 2 * count, stride=16), :] = weight * tangent[c]
        w_ref[pl.ds(3, 2 * count, stride=16), :] = weight
        for i, g in enumerate(groups):
            left = jnp.concatenate([w_ref[pl.ds((2 * i + h) * 16, 16), :] for h in range(2)], axis=1)
            total = add_parts(dot_nt(three_parts(left), jnp.concatenate(own_hot[g], axis=1)))
            d_ref[pl.ds(8 * i, 8), :] = total[:8]
        inv = 1.0 / (d_ref[pl.ds(3, count, stride=8), :] + 1.0)
        delta = [d_ref[pl.ds(c, count, stride=8), :] * inv for c in range(3)]
        return mat_mul(current, exp_rotation(delta))

    parts = [three_parts(e_ref[pl.ds(16 * i, 16), :]) for i in range(5)]
    current = [e_ref[pl.ds(16 + c, 3, stride=16), :] for c in range(9)]
    middle = sweep(parts, [0, 1, 2], relative, live, current)
    for c in range(9):
        e_ref[pl.ds(c, 3, stride=16), :] = middle[c]
    parts = [three_parts(e_ref[pl.ds(16 * i, 16), :]) for i in range(3)]
    final = sweep(parts, [1], [r[2:4] for r in relative], live[2:4], [m[1:2] for m in middle])
    for c in range(9):
        rot_ref[pl.ds(c, 1), :] = final[c]


def sweeps(got):
    vmem = pl.BlockSpec(memory_space=pltpu.VMEM)
    return pl.pallas_call(
        sweep_kernel,
        out_shape=(jax.ShapeDtypeStruct((6, 256), F32), jax.ShapeDtypeStruct((9, LANES), F32)),
        in_specs=[vmem],
        out_specs=(vmem, vmem),
        scratch_shapes=[
            pltpu.VMEM((256, LANES), F32),
            pltpu.VMEM((64, LANES), F32),
            pltpu.VMEM((64, LANES), F32),
            pltpu.VMEM((144, LANES), F32),
            pltpu.VMEM((128, LANES), F32),
            pltpu.VMEM((128, LANES), F32),
            pltpu.VMEM((128, LANES), F32),
            pltpu.VMEM((64, LANES), F32),
        ],
        compiler_params=pltpu.CompilerParams(vmem_limit_bytes=8 * 1024 * 1024),
        cost_estimate=pl.CostEstimate(flops=60_000_000, bytes_accessed=200_000, transcendentals=0),
        name="sweeps",
    )(got)


def on_device(points, offsets, normals, block_count, block_edge, edge_scan, edge_nbr, rotvec):
    terms = block_terms(
        points,
        offsets,
        normals,
        block_count.reshape(8, LANES),
        block_edge.reshape(8, LANES),
        edge_scan.reshape(2, LANES),
        edge_nbr.reshape(2, LANES),
        rotvec,
    )
    moved = lax.all_to_all(terms, AXES, split_axis=0, concat_axis=0, tiled=True)
    solved = pair_solve(moved)
    returned = lax.all_to_all(solved, AXES, split_axis=0, concat_axis=0, tiled=True)
    return sweeps(returned)


def solution(mesh):
    placed = (
        P(None, AXES, None),
        P(None, AXES, None),
        P(None, AXES, None),
        P(AXES),
        P(AXES),
        P(AXES),
        P(AXES),
        P(None, AXES),
    )
    return jax.shard_map(
        on_device,
        mesh=mesh,
        in_specs=placed,
        out_specs=(P(None, AXES), P(None, AXES)),
        check_vma=False,
    )
```

```python
import jax
import jax.numpy as jnp
from jax import lax
from jax.experimental import pallas as pl
from jax.experimental.pallas import tpu as pltpu
from jax.sharding import PartitionSpec as P

DAMPING = 16.0
MIN_LENGTH = 0.1
LANES = 128
TILES = 8
CHUNK_TILES = (2, 3, 3)
AXES = ("region", "pair")
F32 = jnp.float32
BF16 = jnp.bfloat16

UPPER = [(a, b) for a in range(6) for b in range(a, 6)]
SLOT_OF = {pair: i for i, pair in enumerate(UPPER)}
N_TERMS = 27
ROW_FILL = 27
ROW_EDGE = 28
PACK_LANES = (29, 30, 31, 61, 62, 63, 93)
GROUP = 24
STEPS = (-32, -16, 0, 16, 32)


def three_parts(x):
    high = x.astype(BF16).astype(F32)
    rest = x - high
    mid = rest.astype(BF16).astype(F32)
    return jnp.concatenate([high, mid, rest - mid], axis=0).astype(BF16)


def add_parts(x):
    n = x.shape[0] // 3
    return x[:n] + x[n : 2 * n] + x[2 * n :]


def dot_nn(a, b):
    return lax.dot_general(a, b, (((1,), (0,)), ((), ())), preferred_element_type=F32)


def dot_nt(a, b):
    return lax.dot_general(a, b, (((1,), (1,)), ((), ())), preferred_element_type=F32)


def terms_kernel(cnt_hbm, edge_hbm, scan_hbm, nbr_hbm, vec_hbm, p_hbm, d_hbm, n_hbm, out_ref, cnt_ref, edge_ref, scan_ref, nbr_ref, vec_ref, pack_ref, pbuf, dbuf, nbuf, sum_ref, t_ref, sems, id_sems, *tr_refs):
    def chunk_copies(i):
        rows = pl.ds(sum(CHUNK_TILES[:i]) * LANES, CHUNK_TILES[i] * LANES)
        pairs = ((p_hbm, pbuf), (d_hbm, dbuf), (n_hbm, nbuf))
        return [pltpu.make_async_copy(src.at[:, rows, :], dst.at[:, rows, :], sems.at[a, i]) for a, (src, dst) in enumerate(pairs)]

    small = ((cnt_hbm, cnt_ref), (edge_hbm, edge_ref), (scan_hbm, scan_ref), (nbr_hbm, nbr_ref), (vec_hbm, vec_ref))
    id_copies = [pltpu.make_async_copy(src, dst, id_sems.at[i]) for i, (src, dst) in enumerate(small)]
    id_copies[0].start()
    for i in range(len(CHUNK_TILES)):
        for c in chunk_copies(i):
            c.start()
        if i == 0:
            for c in id_copies[1:]:
                c.start()
    sub = lax.broadcasted_iota(jnp.int32, (8, LANES), 0)
    fourth = lax.broadcasted_iota(jnp.int32, (32, LANES), 1) % 4
    pack_ref[...] = jnp.zeros_like(pack_ref)
    id_copies[0].wait()

    def lay_out_pack():
        pack = [vec_ref[pl.ds(c, 1), :] for c in range(3)]
        pack += [ids[pl.ds(h, 1), :].astype(F32) for ids in (scan_ref, nbr_ref) for h in range(2)]
        for lane, row in zip(PACK_LANES, pack):
            pack_ref[pl.ds(lane, 1), :] = row
        pack_ref[...] = pack_ref[...].T

    def turn(t, tr):
        at = pl.ds(t * LANES, LANES)
        for c in range(3):
            tr[c] = pbuf[c, at, :].T
        n = [nbuf[c, at, :] for c in range(3)]
        for c in range(3):
            tr[3 + c] = n[c].T
        tr[6] = (n[0] * dbuf[0, at, :] + n[1] * dbuf[1, at, :] + n[2] * dbuf[2, at, :]).T

    def products(t, tr):
        cnt = cnt_ref[pl.ds(t, 1), :]
        acc = [None] * N_TERMS
        for r in range(LANES // 8):
            at = pl.ds(8 * r, 8)
            keep = (sub + 8 * r) < cnt
            p = [tr[c, at, :] for c in range(3)]
            n = [jnp.where(keep, tr[3 + c, at, :], 0.0) for c in range(3)]
            jac = [p[1] * n[2] - p[2] * n[1], p[2] * n[0] - p[0] * n[2], p[0] * n[1] - p[1] * n[0]] + n
            resid = tr[6, at, :]
            prods = [jac[a] * jac[b] for a, b in UPPER] + [j * resid for j in jac]
            acc = [x if y is None else y + x for x, y in zip(prods, acc)]
        groups = [fold(fold_halves(acc[8 * g : 8 * g + 8]), 2) for g in range(3)]
        blank = jnp.zeros((8, LANES), F32)
        last = fold(fold_halves(acc[24:27] + [blank] * 5), 2)
        fill = jnp.broadcast_to((cnt > 0).astype(F32), (8, LANES))
        last = jnp.where(sub == ROW_FILL - 24, fill, last)
        sum_ref[pl.ds(32 * t, 32), :] = jnp.concatenate(groups + [last], axis=0)

    def fold_halves(v):
        out = []
        for x, y in zip(v[:4], v[4:]):
            out.append(jnp.where(sub < 4, x, y) + pltpu.roll(jnp.where(sub < 4, y, x), 4, 0))
        return out

    def fold(v, step):
        while step:
            low = sub % (2 * step) < step
            half = len(v) // 2
            v = [
                jnp.where(low, x + pltpu.roll(x, 8 - step, 0), y + pltpu.roll(y, step, 0))
                for x, y in zip(v[:half], v[half:])
            ]
            step //= 2
        return v[0]

    def spread(t):
        sum_ref[pl.ds(32 * t + ROW_EDGE, 1), :] = edge_ref[pl.ds(t, 1), :].astype(F32)
        value = sum_ref[pl.ds(32 * t, 32), :]
        t_ref[t] = jnp.concatenate([jnp.where(fourth == k, value, 0.0) for k in range(4)], axis=0).T

    def send_rows(t):
        for q in range(4):
            value = fold([t_ref[t, pl.ds(32 * q + 8 * o, 8), :] for o in range(4)], 2)
            extra = pack_ref[pl.ds(16 * t + 4 * q, 4), :]
            out_ref[pl.ds(t * 32 + 8 * q, 4, stride=2), :] = value[:4] + extra
            out_ref[pl.ds(t * 32 + 8 * q + 1, 4, stride=2), :] = value[4:]

    def wait_chunk(i):
        for c in chunk_copies(i):
            c.wait()

    for i, tiles in enumerate(CHUNK_TILES):
        wait_chunk(i)
        if i == len(CHUNK_TILES) - 1:
            for c in id_copies[1:]:
                c.wait()
            lay_out_pack()
        for t in range(sum(CHUNK_TILES[:i]), sum(CHUNK_TILES[: i + 1])):
            tr = tr_refs[t % len(tr_refs)]
            turn(t, tr)
            products(t, tr)
    for t in range(TILES):
        spread(t)
    for t in range(TILES):
        send_rows(t)


def block_terms(points, offsets, normals, count, edge, scan, nbr, rotvec):
    hbm = pl.BlockSpec(memory_space=pl.ANY)
    vmem = pl.BlockSpec(memory_space=pltpu.VMEM)
    return pl.pallas_call(
        terms_kernel,
        out_shape=jax.ShapeDtypeStruct((256, LANES), F32),
        in_specs=[hbm] * 8,
        out_specs=vmem,
        scratch_shapes=[
            pltpu.VMEM((8, LANES), jnp.int32),
            pltpu.VMEM((8, LANES), jnp.int32),
            pltpu.VMEM((2, LANES), jnp.int32),
            pltpu.VMEM((2, LANES), jnp.int32),
            pltpu.VMEM((3, LANES), F32),
            pltpu.VMEM((LANES, LANES), F32),
            pltpu.VMEM((3, 1024, LANES), F32),
            pltpu.VMEM((3, 1024, LANES), F32),
            pltpu.VMEM((3, 1024, LANES), F32),
            pltpu.VMEM((32 * TILES, LANES), F32),
            pltpu.VMEM((TILES, LANES, LANES), F32),
            pltpu.SemaphoreType.DMA((3, len(CHUNK_TILES))),
            pltpu.SemaphoreType.DMA((5,)),
        ]
        + [pltpu.VMEM((7, LANES, LANES), F32)] * 4,
        compiler_params=pltpu.CompilerParams(vmem_limit_bytes=60 * 1024 * 1024),
        cost_estimate=pl.CostEstimate(flops=9_000_000, bytes_accessed=5_000_000, transcendentals=0),
        name="block_terms",
    )(count, edge, scan, nbr, rotvec, points, offsets, normals)


def solve_six(hess, rhs):
    low = {}
    inv = []
    work = dict(hess)
    z = list(rhs)
    for c in range(6):
        inv.append(1.0 / work[c, c])
        for r in range(c + 1, 6):
            low[r, c] = work[c, r] * inv[c]
        for a in range(c + 1, 6):
            for b in range(a, 6):
                work[a, b] = work[a, b] - low[a, c] * work[c, b]
            z[a] = z[a] - low[a, c] * z[c]
    x = [None] * 6
    for r in range(5, -1, -1):
        v = z[r] * inv[r]
        for k in range(r + 1, 6):
            v = v - low[k, r] * x[k]
        x[r] = v
    return x


def solve_kernel(in_ref, out_ref, s_ref, q_ref):
    row = lax.broadcasted_iota(jnp.int32, (256, LANES), 0)
    wanted = ((row % LANES) * 2 + row // LANES).astype(F32)
    lhs, hot = [], []
    for h in range(2):
        got = in_ref[pl.ds(h, LANES, stride=2), :].T
        if h == 0:
            pack = [got[lane : lane + 1] for lane in PACK_LANES]
        for k in range(4):
            part = got[32 * k : 32 * k + 32]
            lhs.append(part)
            hot.append((wanted == part[ROW_EDGE : ROW_EDGE + 1]).astype(F32).astype(BF16))
    lhs = three_parts(jnp.concatenate(lhs, axis=1))
    sums = add_parts(dot_nt(lhs, jnp.concatenate(hot, axis=1)))
    s_ref[pl.ds(0, 32), :] = sums[:, :LANES]
    s_ref[pl.ds(32, 32), :] = sums[:, LANES:]
    term = [s_ref[pl.ds(c, 2, stride=32), :] for c in range(ROW_FILL + 1)]
    hess = {}
    for (a, b), i in SLOT_OF.items():
        hess[a, b] = term[i] + DAMPING if a == b else term[i]
    x = solve_six(hess, term[21:27])
    middle = GROUP * 2
    q_ref[...] = jnp.zeros_like(q_ref)
    for c in range(6):
        q_ref[pl.ds(middle + c, 2, stride=8), :] = -x[c]
    q_ref[pl.ds(middle + 6, 2, stride=8), :] = (term[ROW_FILL] > 0.5).astype(F32)
    for r, row in enumerate(pack):
        q_ref[pl.ds(middle + 16 + r, 1), :] = row
    own = q_ref[pl.ds(middle, GROUP), :]
    for g, step in enumerate(STEPS):
        if step:
            q_ref[pl.ds(GROUP * g, GROUP), :] = pltpu.roll(own, -step % LANES, 1)
    out_ref[...] = q_ref[...].T


def pair_solve(got):
    vmem = pl.BlockSpec(memory_space=pltpu.VMEM)
    return pl.pallas_call(
        solve_kernel,
        out_shape=jax.ShapeDtypeStruct((LANES, LANES), F32),
        in_specs=[vmem],
        out_specs=vmem,
        scratch_shapes=[pltpu.VMEM((256, LANES), F32), pltpu.VMEM((LANES, LANES), F32)],
        compiler_params=pltpu.CompilerParams(vmem_limit_bytes=8 * 1024 * 1024),
        cost_estimate=pl.CostEstimate(flops=50_000_000, bytes_accessed=200_000, transcendentals=0),
        name="pair_solve",
    )(got)


def exp_rotation(v):
    t = v[0] * v[0] + v[1] * v[1] + v[2] * v[2]
    first = 1.0 + t * (-1.0 / 6.0 + t * (1.0 / 120.0 + t * (-1.0 / 5040.0 + t * (1.0 / 362880.0))))
    second = 0.5 + t * (-1.0 / 24.0 + t * (1.0 / 720.0 + t * (-1.0 / 40320.0 + t * (1.0 / 3628800.0))))
    skew = [[None, -v[2], v[1]], [v[2], None, -v[0]], [-v[1], v[0], None]]
    out = []
    for a in range(3):
        for b in range(3):
            value = second * v[a] * v[b]
            value = value + (1.0 - second * t) if a == b else value + first * skew[a][b]
            out.append(value)
    return out


def mat_mul(x, y):
    return [x[3 * a] * y[c] + x[3 * a + 1] * y[3 + c] + x[3 * a + 2] * y[6 + c] for a in range(3) for c in range(3)]


def mat_tmul(x, y):
    return [x[a] * y[c] + x[3 + a] * y[3 + c] + x[6 + a] * y[6 + c] for a in range(3) for c in range(3)]


def angle_of(sine, cosine):
    size = jnp.abs(cosine)
    big = jnp.maximum(sine, size)
    small = jnp.minimum(sine, size)
    shift = small > 0.4142135623730950 * big
    top = jnp.where(shift, small - big, small)
    bottom = jnp.where(shift, small + big, big)
    x = top / jnp.maximum(bottom, 1e-30)
    z = x * x
    poly = ((8.05374449538e-2 * z - 1.38776856032e-1) * z + 1.99777106478e-1) * z - 3.33329491539e-1
    y = poly * z * x + x
    y = jnp.where(shift, y + 0.7853981633974483, y)
    y = jnp.where(sine > size, 1.5707963267948966 - y, y)
    return jnp.where(cosine < 0.0, 3.141592653589793 - y, y)


def log_rotation(m):
    cosine = (m[0] + m[4] + m[8] - 1.0) * 0.5
    u = [0.5 * (m[7] - m[5]), 0.5 * (m[2] - m[6]), 0.5 * (m[3] - m[1])]
    sine_sq = u[0] * u[0] + u[1] * u[1] + u[2] * u[2]
    sine = jnp.sqrt(sine_sq)
    theta = angle_of(sine, cosine)
    factor = jnp.where(sine < 0.0001, 1.0 + sine_sq / 6.0, theta / jnp.maximum(sine, 0.0001))
    return [factor * u[0], factor * u[1], factor * u[2]]


def sweep_kernel(in_ref, pose_ref, rot_ref, two_ref, s_ref, x_ref, e_ref, n_ref, m_ref, w_ref, d_ref):
    got = in_ref[...]
    two_ref[pl.ds(0, LANES, stride=2), :] = got
    two_ref[pl.ds(1, LANES, stride=2), :] = pltpu.roll(got, LANES - 8, 1)
    for h in range(2):
        part = two_ref[pl.ds(h * LANES, LANES), :].T
        for g in range(3):
            first = GROUP * (g + 1)
            s_ref[pl.ds(16 * g + 8 * h, 8), :] = part[first : first + 8]
        pose_ref[:, h * LANES : (h + 1) * LANES] = part[2 * GROUP : 2 * GROUP + 6]
    relative = exp_rotation([s_ref[pl.ds(c, 6, stride=8), :] for c in range(3)])
    live = s_ref[pl.ds(6, 6, stride=8), :]

    packs = got.T
    for i in range(5):
        x_ref[pl.ds(8 * i, 8), :] = packs[GROUP * i + 16 : GROUP * i + 24]
    start = exp_rotation([x_ref[pl.ds(c, 5, stride=8), :] for c in range(3)])
    e_ref[...] = jnp.zeros_like(e_ref)
    for c in range(9):
        e_ref[pl.ds(c, 5, stride=16), :] = start[c]
    w_ref[...] = jnp.zeros_like(w_ref)

    scan = lax.broadcasted_iota(jnp.int32, (LANES, 2 * LANES), 0).astype(F32)
    near_scan = lax.broadcasted_iota(jnp.int32, (3 * LANES, 2 * LANES), 0).astype(F32)
    own_hot, near_hot = [], []
    for g in range(3):
        ids = x_ref[pl.ds(8 * (g + 1), 8), :]
        own_ids = jnp.concatenate([ids[3:4], ids[4:5]], axis=1)
        near_ids = jnp.concatenate([ids[5:6], ids[6:7]], axis=1)
        own_hot.append((scan == own_ids).astype(F32).astype(BF16))
        near_hot.append((near_scan == near_ids).astype(F32).astype(BF16))

    def sweep(parts, groups, relative, live, current):
        count = len(groups)
        for i, g in enumerate(groups):
            around = jnp.concatenate(parts[i : i + 3], axis=1)
            for ref, got in ((n_ref, dot_nn(around, near_hot[g])), (m_ref, dot_nn(parts[i + 1], own_hot[g]))):
                got = add_parts(got)
                for h in range(2):
                    ref[pl.ds((2 * i + h) * 16, 16), :] = got[:, h * LANES : (h + 1) * LANES]
        near = [n_ref[pl.ds(c, 2 * count, stride=16), :] for c in range(9)]
        mine = [m_ref[pl.ds(c, 2 * count, stride=16), :] for c in range(9)]
        tangent = log_rotation(mat_tmul(mine, mat_mul(near, relative)))
        length = jnp.sqrt(tangent[0] * tangent[0] + tangent[1] * tangent[1] + tangent[2] * tangent[2])
        weight = live / jnp.maximum(length, MIN_LENGTH)
        for c in range(3):
            w_ref[pl.ds(c, 2 * count, stride=16), :] = weight * tangent[c]
        w_ref[pl.ds(3, 2 * count, stride=16), :] = weight
        for i, g in enumerate(groups):
            left = jnp.concatenate([w_ref[pl.ds((2 * i + h) * 16, 16), :] for h in range(2)], axis=1)
            total = add_parts(dot_nt(three_parts(left), own_hot[g]))
            d_ref[pl.ds(8 * i, 8), :] = total[:8]
        inv = 1.0 / (d_ref[pl.ds(3, count, stride=8), :] + 1.0)
        delta = [d_ref[pl.ds(c, count, stride=8), :] * inv for c in range(3)]
        return mat_mul(current, exp_rotation(delta))

    parts = [three_parts(e_ref[pl.ds(16 * i, 16), :]) for i in range(5)]
    current = [e_ref[pl.ds(16 + c, 3, stride=16), :] for c in range(9)]
    middle = sweep(parts, [0, 1, 2], relative, live, current)
    for c in range(9):
        e_ref[pl.ds(c, 3, stride=16), :] = middle[c]
    parts = [three_parts(e_ref[pl.ds(16 * i, 16), :]) for i in range(3)]
    final = sweep(parts, [1], [r[2:4] for r in relative], live[2:4], [m[1:2] for m in middle])
    for c in range(9):
        rot_ref[pl.ds(c, 1), :] = final[c]


def sweeps(got):
    vmem = pl.BlockSpec(memory_space=pltpu.VMEM)
    return pl.pallas_call(
        sweep_kernel,
        out_shape=(jax.ShapeDtypeStruct((6, 256), F32), jax.ShapeDtypeStruct((9, LANES), F32)),
        in_specs=[vmem],
        out_specs=(vmem, vmem),
        scratch_shapes=[
            pltpu.VMEM((256, LANES), F32),
            pltpu.VMEM((64, LANES), F32),
            pltpu.VMEM((64, LANES), F32),
            pltpu.VMEM((144, LANES), F32),
            pltpu.VMEM((128, LANES), F32),
            pltpu.VMEM((128, LANES), F32),
            pltpu.VMEM((128, LANES), F32),
            pltpu.VMEM((64, LANES), F32),
        ],
        compiler_params=pltpu.CompilerParams(vmem_limit_bytes=8 * 1024 * 1024),
        cost_estimate=pl.CostEstimate(flops=60_000_000, bytes_accessed=200_000, transcendentals=0),
        name="sweeps",
    )(got)


def on_device(points, offsets, normals, block_count, block_edge, edge_scan, edge_nbr, rotvec):
    terms = block_terms(
        points,
        offsets,
        normals,
        block_count.reshape(8, LANES),
        block_edge.reshape(8, LANES),
        edge_scan.reshape(2, LANES),
        edge_nbr.reshape(2, LANES),
        rotvec,
    )
    moved = lax.all_to_all(terms, AXES, split_axis=0, concat_axis=0, tiled=True)
    solved = pair_solve(moved)
    returned = lax.all_to_all(solved, AXES, split_axis=0, concat_axis=0, tiled=True)
    return sweeps(returned)


def solution(mesh):
    placed = (
        P(None, AXES, None),
        P(None, AXES, None),
        P(None, AXES, None),
        P(AXES),
        P(AXES),
        P(AXES),
        P(AXES),
        P(None, AXES),
    )
    return jax.shard_map(
        on_device,
        mesh=mesh,
        in_specs=placed,
        out_specs=(P(None, AXES), P(None, AXES)),
        check_vma=False,
    )
```

```python
import jax
import jax.numpy as jnp
from jax import lax
from jax.experimental import pallas as pl
from jax.experimental.pallas import tpu as pltpu
from jax.sharding import PartitionSpec as P

DAMPING = 16.0
MIN_LENGTH = 0.1
LANES = 128
TILES = 8
CHUNK_TILES = (2, 3, 3)
AXES = ("region", "pair")
F32 = jnp.float32
BF16 = jnp.bfloat16

UPPER = [(a, b) for a in range(6) for b in range(a, 6)]
SLOT_OF = {pair: i for i, pair in enumerate(UPPER)}
N_TERMS = 27
ROW_FILL = 27
ROW_EDGE = 28
PACK_LANES = (29, 30, 31, 61, 62, 63, 93)
GROUP = 24
STEPS = (-32, -16, 0, 16, 32)


def three_parts(x):
    high = x.astype(BF16).astype(F32)
    rest = x - high
    mid = rest.astype(BF16).astype(F32)
    return jnp.concatenate([high, mid, rest - mid], axis=0).astype(BF16)


def add_parts(x):
    n = x.shape[0] // 3
    return x[:n] + x[n : 2 * n] + x[2 * n :]


def dot_nn(a, b):
    return lax.dot_general(a, b, (((1,), (0,)), ((), ())), preferred_element_type=F32)


def dot_nt(a, b):
    return lax.dot_general(a, b, (((1,), (1,)), ((), ())), preferred_element_type=F32)


def terms_kernel(cnt_hbm, edge_hbm, scan_hbm, nbr_hbm, vec_hbm, p_hbm, d_hbm, n_hbm, out_ref, cnt_ref, edge_ref, scan_ref, nbr_ref, vec_ref, pack_ref, pbuf, dbuf, nbuf, sum_ref, t_ref, sems, id_sems, *tr_refs):
    def chunk_copies(i):
        rows = pl.ds(sum(CHUNK_TILES[:i]) * LANES, CHUNK_TILES[i] * LANES)
        pairs = ((p_hbm, pbuf), (d_hbm, dbuf), (n_hbm, nbuf))
        return [pltpu.make_async_copy(src.at[:, rows, :], dst.at[:, rows, :], sems.at[a, i]) for a, (src, dst) in enumerate(pairs)]

    small = ((cnt_hbm, cnt_ref), (edge_hbm, edge_ref), (scan_hbm, scan_ref), (nbr_hbm, nbr_ref), (vec_hbm, vec_ref))
    id_copies = [pltpu.make_async_copy(src, dst, id_sems.at[i]) for i, (src, dst) in enumerate(small)]
    id_copies[0].start()
    for i in range(len(CHUNK_TILES)):
        for c in chunk_copies(i):
            c.start()
        if i == 0:
            for c in id_copies[1:]:
                c.start()
    sub = lax.broadcasted_iota(jnp.int32, (8, LANES), 0)
    fourth = lax.broadcasted_iota(jnp.int32, (32, LANES), 1) % 4
    pack_ref[...] = jnp.zeros_like(pack_ref)
    id_copies[0].wait()

    def lay_out_pack():
        pack = [vec_ref[pl.ds(c, 1), :] for c in range(3)]
        pack += [ids[pl.ds(h, 1), :].astype(F32) for ids in (scan_ref, nbr_ref) for h in range(2)]
        for lane, row in zip(PACK_LANES, pack):
            pack_ref[pl.ds(lane, 1), :] = row
        pack_ref[...] = pack_ref[...].T

    def turn(t, tr):
        at = pl.ds(t * LANES, LANES)
        for c in range(3):
            tr[c] = pbuf[c, at, :].T
        n = [nbuf[c, at, :] for c in range(3)]
        for c in range(3):
            tr[3 + c] = n[c].T
        tr[6] = (n[0] * dbuf[0, at, :] + n[1] * dbuf[1, at, :] + n[2] * dbuf[2, at, :]).T

    def products(t, tr):
        cnt = cnt_ref[pl.ds(t, 1), :]
        acc = [None] * N_TERMS
        for r in range(LANES // 8):
            at = pl.ds(8 * r, 8)
            keep = (sub + 8 * r) < cnt
            p = [tr[c, at, :] for c in range(3)]
            n = [jnp.where(keep, tr[3 + c, at, :], 0.0) for c in range(3)]
            jac = [p[1] * n[2] - p[2] * n[1], p[2] * n[0] - p[0] * n[2], p[0] * n[1] - p[1] * n[0]] + n
            resid = tr[6, at, :]
            prods = [jac[a] * jac[b] for a, b in UPPER] + [j * resid for j in jac]
            acc = [x if y is None else y + x for x, y in zip(prods, acc)]
        groups = [fold(fold_halves(acc[8 * g : 8 * g + 8]), 2) for g in range(3)]
        blank = jnp.zeros((8, LANES), F32)
        last = fold(fold_halves(acc[24:27] + [blank] * 5), 2)
        fill = jnp.broadcast_to((cnt > 0).astype(F32), (8, LANES))
        last = jnp.where(sub == ROW_FILL - 24, fill, last)
        sum_ref[pl.ds(32 * t, 32), :] = jnp.concatenate(groups + [last], axis=0)

    def fold_halves(v):
        out = []
        for x, y in zip(v[:4], v[4:]):
            out.append(jnp.where(sub < 4, x, y) + pltpu.roll(jnp.where(sub < 4, y, x), 4, 0))
        return out

    def fold(v, step):
        while step:
            low = sub % (2 * step) < step
            half = len(v) // 2
            v = [
                jnp.where(low, x + pltpu.roll(x, 8 - step, 0), y + pltpu.roll(y, step, 0))
                for x, y in zip(v[:half], v[half:])
            ]
            step //= 2
        return v[0]

    def spread(t):
        sum_ref[pl.ds(32 * t + ROW_EDGE, 1), :] = edge_ref[pl.ds(t, 1), :].astype(F32)
        value = sum_ref[pl.ds(32 * t, 32), :]
        t_ref[t] = jnp.concatenate([jnp.where(fourth == k, value, 0.0) for k in range(4)], axis=0).T

    def send_rows(t):
        for q in range(2):
            left, right = (fold([t_ref[t, pl.ds(64 * q + 32 * i + 8 * o, 8), :] for o in range(4)], 2) for i in range(2))
            first = jnp.where(sub < 4, left, pltpu.roll(right, 4, 0))
            second = jnp.where(sub < 4, pltpu.roll(left, 4, 0), right)
            extra = pack_ref[pl.ds(16 * t + 8 * q, 8), :]
            out_ref[pl.ds(t * 32 + 16 * q, 8, stride=2), :] = first + extra
            out_ref[pl.ds(t * 32 + 16 * q + 1, 8, stride=2), :] = second

    def wait_chunk(i):
        for c in chunk_copies(i):
            c.wait()

    for i, tiles in enumerate(CHUNK_TILES):
        wait_chunk(i)
        if i == len(CHUNK_TILES) - 1:
            for c in id_copies[1:]:
                c.wait()
            lay_out_pack()
        for t in range(sum(CHUNK_TILES[:i]), sum(CHUNK_TILES[: i + 1])):
            tr = tr_refs[t % len(tr_refs)]
            turn(t, tr)
            products(t, tr)
    for t in range(TILES):
        spread(t)
    for t in range(TILES):
        send_rows(t)


def block_terms(points, offsets, normals, count, edge, scan, nbr, rotvec):
    hbm = pl.BlockSpec(memory_space=pl.ANY)
    vmem = pl.BlockSpec(memory_space=pltpu.VMEM)
    return pl.pallas_call(
        terms_kernel,
        out_shape=jax.ShapeDtypeStruct((256, LANES), F32),
        in_specs=[hbm] * 8,
        out_specs=vmem,
        scratch_shapes=[
            pltpu.VMEM((8, LANES), jnp.int32),
            pltpu.VMEM((8, LANES), jnp.int32),
            pltpu.VMEM((2, LANES), jnp.int32),
            pltpu.VMEM((2, LANES), jnp.int32),
            pltpu.VMEM((3, LANES), F32),
            pltpu.VMEM((LANES, LANES), F32),
            pltpu.VMEM((3, 1024, LANES), F32),
            pltpu.VMEM((3, 1024, LANES), F32),
            pltpu.VMEM((3, 1024, LANES), F32),
            pltpu.VMEM((32 * TILES, LANES), F32),
            pltpu.VMEM((TILES, LANES, LANES), F32),
            pltpu.SemaphoreType.DMA((3, len(CHUNK_TILES))),
            pltpu.SemaphoreType.DMA((5,)),
        ]
        + [pltpu.VMEM((7, LANES, LANES), F32)] * 4,
        compiler_params=pltpu.CompilerParams(vmem_limit_bytes=60 * 1024 * 1024),
        cost_estimate=pl.CostEstimate(flops=9_000_000, bytes_accessed=5_000_000, transcendentals=0),
        name="block_terms",
    )(count, edge, scan, nbr, rotvec, points, offsets, normals)


def solve_six(hess, rhs):
    low = {}
    inv = []
    work = dict(hess)
    z = list(rhs)
    for c in range(6):
        inv.append(1.0 / work[c, c])
        for r in range(c + 1, 6):
            low[r, c] = work[c, r] * inv[c]
        for a in range(c + 1, 6):
            for b in range(a, 6):
                work[a, b] = work[a, b] - low[a, c] * work[c, b]
            z[a] = z[a] - low[a, c] * z[c]
    x = [None] * 6
    for r in range(5, -1, -1):
        v = z[r] * inv[r]
        for k in range(r + 1, 6):
            v = v - low[k, r] * x[k]
        x[r] = v
    return x


def solve_kernel(in_ref, out_ref, s_ref, q_ref):
    row = lax.broadcasted_iota(jnp.int32, (256, LANES), 0)
    wanted = ((row % LANES) * 2 + row // LANES).astype(F32)
    lhs, hot = [], []
    for h in range(2):
        got = in_ref[pl.ds(h, LANES, stride=2), :].T
        if h == 0:
            pack = [got[lane : lane + 1] for lane in PACK_LANES]
        for k in range(4):
            part = got[32 * k : 32 * k + 32]
            lhs.append(part)
            hot.append((wanted == part[ROW_EDGE : ROW_EDGE + 1]).astype(F32).astype(BF16))
    lhs = three_parts(jnp.concatenate(lhs, axis=1))
    sums = add_parts(dot_nt(lhs, jnp.concatenate(hot, axis=1)))
    s_ref[pl.ds(0, 32), :] = sums[:, :LANES]
    s_ref[pl.ds(32, 32), :] = sums[:, LANES:]
    term = [s_ref[pl.ds(c, 2, stride=32), :] for c in range(ROW_FILL + 1)]
    hess = {}
    for (a, b), i in SLOT_OF.items():
        hess[a, b] = term[i] + DAMPING if a == b else term[i]
    x = solve_six(hess, term[21:27])
    middle = GROUP * 2
    q_ref[...] = jnp.zeros_like(q_ref)
    for c in range(6):
        q_ref[pl.ds(middle + c, 2, stride=8), :] = -x[c]
    q_ref[pl.ds(middle + 6, 2, stride=8), :] = (term[ROW_FILL] > 0.5).astype(F32)
    for r, row in enumerate(pack):
        q_ref[pl.ds(middle + 16 + r, 1), :] = row
    own = q_ref[pl.ds(middle, GROUP), :]
    for g, step in enumerate(STEPS):
        if step:
            q_ref[pl.ds(GROUP * g, GROUP), :] = pltpu.roll(own, -step % LANES, 1)
    out_ref[...] = q_ref[...].T


def pair_solve(got):
    vmem = pl.BlockSpec(memory_space=pltpu.VMEM)
    return pl.pallas_call(
        solve_kernel,
        out_shape=jax.ShapeDtypeStruct((LANES, LANES), F32),
        in_specs=[vmem],
        out_specs=vmem,
        scratch_shapes=[pltpu.VMEM((256, LANES), F32), pltpu.VMEM((LANES, LANES), F32)],
        compiler_params=pltpu.CompilerParams(vmem_limit_bytes=8 * 1024 * 1024),
        cost_estimate=pl.CostEstimate(flops=50_000_000, bytes_accessed=200_000, transcendentals=0),
        name="pair_solve",
    )(got)


def exp_rotation(v):
    t = v[0] * v[0] + v[1] * v[1] + v[2] * v[2]
    first = 1.0 + t * (-1.0 / 6.0 + t * (1.0 / 120.0 + t * (-1.0 / 5040.0 + t * (1.0 / 362880.0))))
    second = 0.5 + t * (-1.0 / 24.0 + t * (1.0 / 720.0 + t * (-1.0 / 40320.0 + t * (1.0 / 3628800.0))))
    skew = [[None, -v[2], v[1]], [v[2], None, -v[0]], [-v[1], v[0], None]]
    out = []
    for a in range(3):
        for b in range(3):
            value = second * v[a] * v[b]
            value = value + (1.0 - second * t) if a == b else value + first * skew[a][b]
            out.append(value)
    return out


def mat_mul(x, y):
    return [x[3 * a] * y[c] + x[3 * a + 1] * y[3 + c] + x[3 * a + 2] * y[6 + c] for a in range(3) for c in range(3)]


def mat_tmul(x, y):
    return [x[a] * y[c] + x[3 + a] * y[3 + c] + x[6 + a] * y[6 + c] for a in range(3) for c in range(3)]


def angle_of(sine, cosine):
    size = jnp.abs(cosine)
    big = jnp.maximum(sine, size)
    small = jnp.minimum(sine, size)
    shift = small > 0.4142135623730950 * big
    top = jnp.where(shift, small - big, small)
    bottom = jnp.where(shift, small + big, big)
    x = top / jnp.maximum(bottom, 1e-30)
    z = x * x
    poly = ((8.05374449538e-2 * z - 1.38776856032e-1) * z + 1.99777106478e-1) * z - 3.33329491539e-1
    y = poly * z * x + x
    y = jnp.where(shift, y + 0.7853981633974483, y)
    y = jnp.where(sine > size, 1.5707963267948966 - y, y)
    return jnp.where(cosine < 0.0, 3.141592653589793 - y, y)


def log_rotation(m):
    cosine = (m[0] + m[4] + m[8] - 1.0) * 0.5
    u = [0.5 * (m[7] - m[5]), 0.5 * (m[2] - m[6]), 0.5 * (m[3] - m[1])]
    sine_sq = u[0] * u[0] + u[1] * u[1] + u[2] * u[2]
    sine = jnp.sqrt(sine_sq)
    theta = angle_of(sine, cosine)
    factor = jnp.where(sine < 0.0001, 1.0 + sine_sq / 6.0, theta / jnp.maximum(sine, 0.0001))
    return [factor * u[0], factor * u[1], factor * u[2]]


def sweep_kernel(in_ref, pose_ref, rot_ref, two_ref, s_ref, x_ref, e_ref, n_ref, m_ref, w_ref, d_ref):
    got = in_ref[...]
    two_ref[pl.ds(0, LANES, stride=2), :] = got
    two_ref[pl.ds(1, LANES, stride=2), :] = pltpu.roll(got, LANES - 8, 1)
    for h in range(2):
        part = two_ref[pl.ds(h * LANES, LANES), :].T
        for g in range(3):
            first = GROUP * (g + 1)
            s_ref[pl.ds(16 * g + 8 * h, 8), :] = part[first : first + 8]
        pose_ref[:, h * LANES : (h + 1) * LANES] = part[2 * GROUP : 2 * GROUP + 6]
    relative = exp_rotation([s_ref[pl.ds(c, 6, stride=8), :] for c in range(3)])
    live = s_ref[pl.ds(6, 6, stride=8), :]

    packs = got.T
    for i in range(5):
        x_ref[pl.ds(8 * i, 8), :] = packs[GROUP * i + 16 : GROUP * i + 24]
    start = exp_rotation([x_ref[pl.ds(c, 5, stride=8), :] for c in range(3)])
    e_ref[...] = jnp.zeros_like(e_ref)
    for c in range(9):
        e_ref[pl.ds(c, 5, stride=16), :] = start[c]
    w_ref[...] = jnp.zeros_like(w_ref)

    scan = lax.broadcasted_iota(jnp.int32, (LANES, 2 * LANES), 0).astype(F32)
    near_scan = lax.broadcasted_iota(jnp.int32, (3 * LANES, 2 * LANES), 0).astype(F32)
    own_hot, near_hot = [], []
    for g in range(3):
        ids = x_ref[pl.ds(8 * (g + 1), 8), :]
        own_ids = jnp.concatenate([ids[3:4], ids[4:5]], axis=1)
        near_ids = jnp.concatenate([ids[5:6], ids[6:7]], axis=1)
        own_hot.append((scan == own_ids).astype(F32).astype(BF16))
        near_hot.append((near_scan == near_ids).astype(F32).astype(BF16))

    def sweep(parts, groups, relative, live, current):
        count = len(groups)
        for i, g in enumerate(groups):
            around = jnp.concatenate(parts[i : i + 3], axis=1)
            for ref, got in ((n_ref, dot_nn(around, near_hot[g])), (m_ref, dot_nn(parts[i + 1], own_hot[g]))):
                got = add_parts(got)
                for h in range(2):
                    ref[pl.ds((2 * i + h) * 16, 16), :] = got[:, h * LANES : (h + 1) * LANES]
        near = [n_ref[pl.ds(c, 2 * count, stride=16), :] for c in range(9)]
        mine = [m_ref[pl.ds(c, 2 * count, stride=16), :] for c in range(9)]
        tangent = log_rotation(mat_tmul(mine, mat_mul(near, relative)))
        length = jnp.sqrt(tangent[0] * tangent[0] + tangent[1] * tangent[1] + tangent[2] * tangent[2])
        weight = live / jnp.maximum(length, MIN_LENGTH)
        for c in range(3):
            w_ref[pl.ds(c, 2 * count, stride=16), :] = weight * tangent[c]
        w_ref[pl.ds(3, 2 * count, stride=16), :] = weight
        for i, g in enumerate(groups):
            left = jnp.concatenate([w_ref[pl.ds((2 * i + h) * 16, 16), :] for h in range(2)], axis=1)
            total = add_parts(dot_nt(three_parts(left), own_hot[g]))
            d_ref[pl.ds(8 * i, 8), :] = total[:8]
        inv = 1.0 / (d_ref[pl.ds(3, count, stride=8), :] + 1.0)
        delta = [d_ref[pl.ds(c, count, stride=8), :] * inv for c in range(3)]
        return mat_mul(current, exp_rotation(delta))

    parts = [three_parts(e_ref[pl.ds(16 * i, 16), :]) for i in range(5)]
    current = [e_ref[pl.ds(16 + c, 3, stride=16), :] for c in range(9)]
    middle = sweep(parts, [0, 1, 2], relative, live, current)
    for c in range(9):
        e_ref[pl.ds(c, 3, stride=16), :] = middle[c]
    parts = [three_parts(e_ref[pl.ds(16 * i, 16), :]) for i in range(3)]
    final = sweep(parts, [1], [r[2:4] for r in relative], live[2:4], [m[1:2] for m in middle])
    for c in range(9):
        rot_ref[pl.ds(c, 1), :] = final[c]


def sweeps(got):
    vmem = pl.BlockSpec(memory_space=pltpu.VMEM)
    return pl.pallas_call(
        sweep_kernel,
        out_shape=(jax.ShapeDtypeStruct((6, 256), F32), jax.ShapeDtypeStruct((9, LANES), F32)),
        in_specs=[vmem],
        out_specs=(vmem, vmem),
        scratch_shapes=[
            pltpu.VMEM((256, LANES), F32),
            pltpu.VMEM((64, LANES), F32),
            pltpu.VMEM((64, LANES), F32),
            pltpu.VMEM((144, LANES), F32),
            pltpu.VMEM((128, LANES), F32),
            pltpu.VMEM((128, LANES), F32),
            pltpu.VMEM((128, LANES), F32),
            pltpu.VMEM((64, LANES), F32),
        ],
        compiler_params=pltpu.CompilerParams(vmem_limit_bytes=8 * 1024 * 1024),
        cost_estimate=pl.CostEstimate(flops=60_000_000, bytes_accessed=200_000, transcendentals=0),
        name="sweeps",
    )(got)


def on_device(points, offsets, normals, block_count, block_edge, edge_scan, edge_nbr, rotvec):
    terms = block_terms(
        points,
        offsets,
        normals,
        block_count.reshape(8, LANES),
        block_edge.reshape(8, LANES),
        edge_scan.reshape(2, LANES),
        edge_nbr.reshape(2, LANES),
        rotvec,
    )
    moved = lax.all_to_all(terms, AXES, split_axis=0, concat_axis=0, tiled=True)
    solved = pair_solve(moved)
    returned = lax.all_to_all(solved, AXES, split_axis=0, concat_axis=0, tiled=True)
    return sweeps(returned)


def solution(mesh):
    placed = (
        P(None, AXES, None),
        P(None, AXES, None),
        P(None, AXES, None),
        P(AXES),
        P(AXES),
        P(AXES),
        P(AXES),
        P(None, AXES),
    )
    return jax.shard_map(
        on_device,
        mesh=mesh,
        in_specs=placed,
        out_specs=(P(None, AXES), P(None, AXES)),
        check_vma=False,
    )
```

```python
import jax
import jax.numpy as jnp
from jax import lax
from jax.experimental import pallas as pl
from jax.experimental.pallas import tpu as pltpu
from jax.sharding import PartitionSpec as P

DAMPING = 16.0
MIN_LENGTH = 0.1
LANES = 128
TILES = 8
CHUNK_TILES = (2, 3, 3)
AXES = ("region", "pair")
F32 = jnp.float32
BF16 = jnp.bfloat16

UPPER = [(a, b) for a in range(6) for b in range(a, 6)]
SLOT_OF = {pair: i for i, pair in enumerate(UPPER)}
N_TERMS = 27
ROW_FILL = 27
ROW_EDGE = 28
PACK_LANES = (29, 30, 31, 61, 62, 63, 93)
GROUP = 24
STEPS = (-32, -16, 0, 16, 32)


def three_parts(x):
    high = x.astype(BF16).astype(F32)
    rest = x - high
    mid = rest.astype(BF16).astype(F32)
    return jnp.concatenate([high, mid, rest - mid], axis=0).astype(BF16)


def add_parts(x):
    n = x.shape[0] // 3
    return x[:n] + x[n : 2 * n] + x[2 * n :]


def dot_nn(a, b):
    return lax.dot_general(a, b, (((1,), (0,)), ((), ())), preferred_element_type=F32)


def dot_nt(a, b):
    return lax.dot_general(a, b, (((1,), (1,)), ((), ())), preferred_element_type=F32)


def terms_kernel(cnt_hbm, edge_hbm, scan_hbm, nbr_hbm, vec_hbm, p_hbm, d_hbm, n_hbm, out_ref, cnt_ref, edge_ref, scan_ref, nbr_ref, vec_ref, pack_ref, pbuf, dbuf, nbuf, sum_ref, t_ref, sems, id_sems, *tr_refs):
    def chunk_copies(i):
        rows = pl.ds(sum(CHUNK_TILES[:i]) * LANES, CHUNK_TILES[i] * LANES)
        pairs = ((p_hbm, pbuf), (d_hbm, dbuf), (n_hbm, nbuf))
        return [pltpu.make_async_copy(src.at[:, rows, :], dst.at[:, rows, :], sems.at[a, i]) for a, (src, dst) in enumerate(pairs)]

    small = ((cnt_hbm, cnt_ref), (edge_hbm, edge_ref), (scan_hbm, scan_ref), (nbr_hbm, nbr_ref), (vec_hbm, vec_ref))
    id_copies = [pltpu.make_async_copy(src, dst, id_sems.at[i]) for i, (src, dst) in enumerate(small)]
    id_copies[0].start()
    for i in range(len(CHUNK_TILES)):
        for c in chunk_copies(i):
            c.start()
        if i == len(CHUNK_TILES) - 1:
            for c in id_copies[1:]:
                c.start()
    sub = lax.broadcasted_iota(jnp.int32, (8, LANES), 0)
    fourth = lax.broadcasted_iota(jnp.int32, (32, LANES), 1) % 4
    pack_ref[...] = jnp.zeros_like(pack_ref)
    id_copies[0].wait()

    def lay_out_pack():
        pack = [vec_ref[pl.ds(c, 1), :] for c in range(3)]
        pack += [ids[pl.ds(h, 1), :].astype(F32) for ids in (scan_ref, nbr_ref) for h in range(2)]
        for lane, row in zip(PACK_LANES, pack):
            pack_ref[pl.ds(lane, 1), :] = row
        pack_ref[...] = pack_ref[...].T

    def turn(t, tr):
        at = pl.ds(t * LANES, LANES)
        for c in range(3):
            tr[c] = pbuf[c, at, :].T
        n = [nbuf[c, at, :] for c in range(3)]
        for c in range(3):
            tr[3 + c] = n[c].T
        tr[6] = (n[0] * dbuf[0, at, :] + n[1] * dbuf[1, at, :] + n[2] * dbuf[2, at, :]).T

    def products(t, tr):
        cnt = cnt_ref[pl.ds(t, 1), :]
        acc = [None] * N_TERMS
        for r in range(LANES // 8):
            at = pl.ds(8 * r, 8)
            keep = (sub + 8 * r) < cnt
            p = [tr[c, at, :] for c in range(3)]
            n = [jnp.where(keep, tr[3 + c, at, :], 0.0) for c in range(3)]
            jac = [p[1] * n[2] - p[2] * n[1], p[2] * n[0] - p[0] * n[2], p[0] * n[1] - p[1] * n[0]] + n
            resid = tr[6, at, :]
            prods = [jac[a] * jac[b] for a, b in UPPER] + [j * resid for j in jac]
            acc = [x if y is None else y + x for x, y in zip(prods, acc)]
        groups = [fold(fold_halves(acc[8 * g : 8 * g + 8]), 2) for g in range(3)]
        blank = jnp.zeros((8, LANES), F32)
        last = fold(fold_halves(acc[24:27] + [blank] * 5), 2)
        fill = jnp.broadcast_to((cnt > 0).astype(F32), (8, LANES))
        last = jnp.where(sub == ROW_FILL - 24, fill, last)
        sum_ref[pl.ds(32 * t, 32), :] = jnp.concatenate(groups + [last], axis=0)

    def fold_halves(v):
        out = []
        for x, y in zip(v[:4], v[4:]):
            out.append(jnp.where(sub < 4, x, y) + pltpu.roll(jnp.where(sub < 4, y, x), 4, 0))
        return out

    def fold(v, step):
        while step:
            low = sub % (2 * step) < step
            half = len(v) // 2
            v = [
                jnp.where(low, x + pltpu.roll(x, 8 - step, 0), y + pltpu.roll(y, step, 0))
                for x, y in zip(v[:half], v[half:])
            ]
            step //= 2
        return v[0]

    def spread(t):
        sum_ref[pl.ds(32 * t + ROW_EDGE, 1), :] = edge_ref[pl.ds(t, 1), :].astype(F32)
        value = sum_ref[pl.ds(32 * t, 32), :]
        t_ref[t] = jnp.concatenate([jnp.where(fourth == k, value, 0.0) for k in range(4)], axis=0).T

    def send_rows(t):
        for q in range(2):
            left, right = (fold([t_ref[t, pl.ds(64 * q + 32 * i + 8 * o, 8), :] for o in range(4)], 2) for i in range(2))
            first = jnp.where(sub < 4, left, pltpu.roll(right, 4, 0))
            second = jnp.where(sub < 4, pltpu.roll(left, 4, 0), right)
            extra = pack_ref[pl.ds(16 * t + 8 * q, 8), :]
            out_ref[pl.ds(t * 32 + 16 * q, 8, stride=2), :] = first + extra
            out_ref[pl.ds(t * 32 + 16 * q + 1, 8, stride=2), :] = second

    def wait_chunk(i):
        for c in chunk_copies(i):
            c.wait()

    for i, tiles in enumerate(CHUNK_TILES):
        wait_chunk(i)
        if i == len(CHUNK_TILES) - 1:
            for c in id_copies[1:]:
                c.wait()
            lay_out_pack()
        for t in range(sum(CHUNK_TILES[:i]), sum(CHUNK_TILES[: i + 1])):
            tr = tr_refs[t % len(tr_refs)]
            turn(t, tr)
            products(t, tr)
    for t in range(TILES):
        spread(t)
    for t in range(TILES):
        send_rows(t)


def block_terms(points, offsets, normals, count, edge, scan, nbr, rotvec):
    hbm = pl.BlockSpec(memory_space=pl.ANY)
    vmem = pl.BlockSpec(memory_space=pltpu.VMEM)
    return pl.pallas_call(
        terms_kernel,
        out_shape=jax.ShapeDtypeStruct((256, LANES), F32),
        in_specs=[hbm] * 8,
        out_specs=vmem,
        scratch_shapes=[
            pltpu.VMEM((8, LANES), jnp.int32),
            pltpu.VMEM((8, LANES), jnp.int32),
            pltpu.VMEM((2, LANES), jnp.int32),
            pltpu.VMEM((2, LANES), jnp.int32),
            pltpu.VMEM((3, LANES), F32),
            pltpu.VMEM((LANES, LANES), F32),
            pltpu.VMEM((3, 1024, LANES), F32),
            pltpu.VMEM((3, 1024, LANES), F32),
            pltpu.VMEM((3, 1024, LANES), F32),
            pltpu.VMEM((32 * TILES, LANES), F32),
            pltpu.VMEM((TILES, LANES, LANES), F32),
            pltpu.SemaphoreType.DMA((3, len(CHUNK_TILES))),
            pltpu.SemaphoreType.DMA((5,)),
        ]
        + [pltpu.VMEM((7, LANES, LANES), F32)] * 4,
        compiler_params=pltpu.CompilerParams(vmem_limit_bytes=60 * 1024 * 1024),
        cost_estimate=pl.CostEstimate(flops=9_000_000, bytes_accessed=5_000_000, transcendentals=0),
        name="block_terms",
    )(count, edge, scan, nbr, rotvec, points, offsets, normals)


def solve_six(hess, rhs):
    low = {}
    inv = []
    work = dict(hess)
    z = list(rhs)
    for c in range(6):
        inv.append(1.0 / work[c, c])
        for r in range(c + 1, 6):
            low[r, c] = work[c, r] * inv[c]
        for a in range(c + 1, 6):
            for b in range(a, 6):
                work[a, b] = work[a, b] - low[a, c] * work[c, b]
            z[a] = z[a] - low[a, c] * z[c]
    x = [None] * 6
    for r in range(5, -1, -1):
        v = z[r] * inv[r]
        for k in range(r + 1, 6):
            v = v - low[k, r] * x[k]
        x[r] = v
    return x


def solve_kernel(in_ref, out_ref, s_ref, q_ref):
    row = lax.broadcasted_iota(jnp.int32, (256, LANES), 0)
    wanted = ((row % LANES) * 2 + row // LANES).astype(F32).astype(BF16)
    lhs, hot = [], []
    for h in range(2):
        got = in_ref[pl.ds(h, LANES, stride=2), :].T
        if h == 0:
            pack = [got[lane : lane + 1] for lane in PACK_LANES]
        for k in range(4):
            part = got[32 * k : 32 * k + 32]
            lhs.append(part)
            edge = jnp.broadcast_to(part[ROW_EDGE : ROW_EDGE + 1], (16, LANES)).astype(BF16)
            edge = jnp.concatenate([edge] * 16, axis=0)
            hot.append(jnp.where(wanted == edge, jnp.ones((), BF16), jnp.zeros((), BF16)))
    lhs = three_parts(jnp.concatenate(lhs, axis=1))
    sums = add_parts(dot_nt(lhs, jnp.concatenate(hot, axis=1)))
    s_ref[pl.ds(0, 32), :] = sums[:, :LANES]
    s_ref[pl.ds(32, 32), :] = sums[:, LANES:]
    term = [s_ref[pl.ds(c, 2, stride=32), :] for c in range(ROW_FILL + 1)]
    hess = {}
    for (a, b), i in SLOT_OF.items():
        hess[a, b] = term[i] + DAMPING if a == b else term[i]
    x = solve_six(hess, term[21:27])
    middle = GROUP * 2
    q_ref[...] = jnp.zeros_like(q_ref)
    for c in range(6):
        q_ref[pl.ds(middle + c, 2, stride=8), :] = -x[c]
    q_ref[pl.ds(middle + 6, 2, stride=8), :] = (term[ROW_FILL] > 0.5).astype(F32)
    for r, row in enumerate(pack):
        q_ref[pl.ds(middle + 16 + r, 1), :] = row
    own = q_ref[pl.ds(middle, GROUP), :]
    for g, step in enumerate(STEPS):
        if step:
            q_ref[pl.ds(GROUP * g, GROUP), :] = pltpu.roll(own, -step % LANES, 1)
    out_ref[...] = q_ref[...].T


def pair_solve(got):
    vmem = pl.BlockSpec(memory_space=pltpu.VMEM)
    return pl.pallas_call(
        solve_kernel,
        out_shape=jax.ShapeDtypeStruct((LANES, LANES), F32),
        in_specs=[vmem],
        out_specs=vmem,
        scratch_shapes=[pltpu.VMEM((256, LANES), F32), pltpu.VMEM((LANES, LANES), F32)],
        compiler_params=pltpu.CompilerParams(vmem_limit_bytes=8 * 1024 * 1024),
        cost_estimate=pl.CostEstimate(flops=50_000_000, bytes_accessed=200_000, transcendentals=0),
        name="pair_solve",
    )(got)


def exp_rotation(v):
    t = v[0] * v[0] + v[1] * v[1] + v[2] * v[2]
    first = 1.0 + t * (-1.0 / 6.0 + t * (1.0 / 120.0 + t * (-1.0 / 5040.0 + t * (1.0 / 362880.0))))
    second = 0.5 + t * (-1.0 / 24.0 + t * (1.0 / 720.0 + t * (-1.0 / 40320.0 + t * (1.0 / 3628800.0))))
    skew = [[None, -v[2], v[1]], [v[2], None, -v[0]], [-v[1], v[0], None]]
    out = []
    for a in range(3):
        for b in range(3):
            value = second * v[a] * v[b]
            value = value + (1.0 - second * t) if a == b else value + first * skew[a][b]
            out.append(value)
    return out


def mat_mul(x, y):
    return [x[3 * a] * y[c] + x[3 * a + 1] * y[3 + c] + x[3 * a + 2] * y[6 + c] for a in range(3) for c in range(3)]


def mat_tmul(x, y):
    return [x[a] * y[c] + x[3 + a] * y[3 + c] + x[6 + a] * y[6 + c] for a in range(3) for c in range(3)]


def angle_of(sine, cosine):
    size = jnp.abs(cosine)
    big = jnp.maximum(sine, size)
    small = jnp.minimum(sine, size)
    shift = small > 0.4142135623730950 * big
    top = jnp.where(shift, small - big, small)
    bottom = jnp.where(shift, small + big, big)
    x = top / jnp.maximum(bottom, 1e-30)
    z = x * x
    poly = ((8.05374449538e-2 * z - 1.38776856032e-1) * z + 1.99777106478e-1) * z - 3.33329491539e-1
    y = poly * z * x + x
    y = jnp.where(shift, y + 0.7853981633974483, y)
    y = jnp.where(sine > size, 1.5707963267948966 - y, y)
    return jnp.where(cosine < 0.0, 3.141592653589793 - y, y)


def log_rotation(m):
    cosine = (m[0] + m[4] + m[8] - 1.0) * 0.5
    u = [0.5 * (m[7] - m[5]), 0.5 * (m[2] - m[6]), 0.5 * (m[3] - m[1])]
    sine_sq = u[0] * u[0] + u[1] * u[1] + u[2] * u[2]
    sine = jnp.sqrt(sine_sq)
    theta = angle_of(sine, cosine)
    factor = jnp.where(sine < 0.0001, 1.0 + sine_sq / 6.0, theta / jnp.maximum(sine, 0.0001))
    return [factor * u[0], factor * u[1], factor * u[2]]


def sweep_kernel(in_ref, pose_ref, rot_ref, two_ref, s_ref, x_ref, e_ref, n_ref, m_ref, w_ref, d_ref):
    got = in_ref[...]
    two_ref[pl.ds(0, LANES, stride=2), :] = got
    two_ref[pl.ds(1, LANES, stride=2), :] = pltpu.roll(got, LANES - 8, 1)
    for h in range(2):
        part = two_ref[pl.ds(h * LANES, LANES), :].T
        for g in range(3):
            first = GROUP * (g + 1)
            s_ref[pl.ds(16 * g + 8 * h, 8), :] = part[first : first + 8]
        pose_ref[:, h * LANES : (h + 1) * LANES] = part[2 * GROUP : 2 * GROUP + 6]
    relative = exp_rotation([s_ref[pl.ds(c, 6, stride=8), :] for c in range(3)])
    live = s_ref[pl.ds(6, 6, stride=8), :]

    packs = got.T
    for i in range(5):
        x_ref[pl.ds(8 * i, 8), :] = packs[GROUP * i + 16 : GROUP * i + 24]
    start = exp_rotation([x_ref[pl.ds(c, 5, stride=8), :] for c in range(3)])
    e_ref[...] = jnp.zeros_like(e_ref)
    for c in range(9):
        e_ref[pl.ds(c, 5, stride=16), :] = start[c]
    w_ref[...] = jnp.zeros_like(w_ref)

    scan = lax.broadcasted_iota(jnp.int32, (LANES, 2 * LANES), 0).astype(F32)
    near_scan = lax.broadcasted_iota(jnp.int32, (3 * LANES, 2 * LANES), 0).astype(F32)
    own_hot, near_hot = [], []
    for g in range(3):
        ids = x_ref[pl.ds(8 * (g + 1), 8), :]
        own_ids = jnp.concatenate([ids[3:4], ids[4:5]], axis=1)
        near_ids = jnp.concatenate([ids[5:6], ids[6:7]], axis=1)
        own_hot.append((scan == own_ids).astype(F32).astype(BF16))
        near_hot.append((near_scan == near_ids).astype(F32).astype(BF16))

    def sweep(parts, groups, relative, live, current):
        count = len(groups)
        for i, g in enumerate(groups):
            around = jnp.concatenate(parts[i : i + 3], axis=1)
            for ref, got in ((n_ref, dot_nn(around, near_hot[g])), (m_ref, dot_nn(parts[i + 1], own_hot[g]))):
                got = add_parts(got)
                for h in range(2):
                    ref[pl.ds((2 * i + h) * 16, 16), :] = got[:, h * LANES : (h + 1) * LANES]
        near = [n_ref[pl.ds(c, 2 * count, stride=16), :] for c in range(9)]
        mine = [m_ref[pl.ds(c, 2 * count, stride=16), :] for c in range(9)]
        tangent = log_rotation(mat_tmul(mine, mat_mul(near, relative)))
        length = jnp.sqrt(tangent[0] * tangent[0] + tangent[1] * tangent[1] + tangent[2] * tangent[2])
        weight = live / jnp.maximum(length, MIN_LENGTH)
        for c in range(3):
            w_ref[pl.ds(c, 2 * count, stride=16), :] = weight * tangent[c]
        w_ref[pl.ds(3, 2 * count, stride=16), :] = weight
        for i, g in enumerate(groups):
            left = jnp.concatenate([w_ref[pl.ds((2 * i + h) * 16, 16), :] for h in range(2)], axis=1)
            total = add_parts(dot_nt(three_parts(left), own_hot[g]))
            d_ref[pl.ds(8 * i, 8), :] = total[:8]
        inv = 1.0 / (d_ref[pl.ds(3, count, stride=8), :] + 1.0)
        delta = [d_ref[pl.ds(c, count, stride=8), :] * inv for c in range(3)]
        return mat_mul(current, exp_rotation(delta))

    parts = [three_parts(e_ref[pl.ds(16 * i, 16), :]) for i in range(5)]
    current = [e_ref[pl.ds(16 + c, 3, stride=16), :] for c in range(9)]
    middle = sweep(parts, [0, 1, 2], relative, live, current)
    for c in range(9):
        e_ref[pl.ds(c, 3, stride=16), :] = middle[c]
    parts = [three_parts(e_ref[pl.ds(16 * i, 16), :]) for i in range(3)]
    final = sweep(parts, [1], [r[2:4] for r in relative], live[2:4], [m[1:2] for m in middle])
    for c in range(9):
        rot_ref[pl.ds(c, 1), :] = final[c]


def sweeps(got):
    vmem = pl.BlockSpec(memory_space=pltpu.VMEM)
    return pl.pallas_call(
        sweep_kernel,
        out_shape=(jax.ShapeDtypeStruct((6, 256), F32), jax.ShapeDtypeStruct((9, LANES), F32)),
        in_specs=[vmem],
        out_specs=(vmem, vmem),
        scratch_shapes=[
            pltpu.VMEM((256, LANES), F32),
            pltpu.VMEM((64, LANES), F32),
            pltpu.VMEM((64, LANES), F32),
            pltpu.VMEM((144, LANES), F32),
            pltpu.VMEM((128, LANES), F32),
            pltpu.VMEM((128, LANES), F32),
            pltpu.VMEM((128, LANES), F32),
            pltpu.VMEM((64, LANES), F32),
        ],
        compiler_params=pltpu.CompilerParams(vmem_limit_bytes=8 * 1024 * 1024),
        cost_estimate=pl.CostEstimate(flops=60_000_000, bytes_accessed=200_000, transcendentals=0),
        name="sweeps",
    )(got)


def on_device(points, offsets, normals, block_count, block_edge, edge_scan, edge_nbr, rotvec):
    terms = block_terms(
        points,
        offsets,
        normals,
        block_count.reshape(8, LANES),
        block_edge.reshape(8, LANES),
        edge_scan.reshape(2, LANES),
        edge_nbr.reshape(2, LANES),
        rotvec,
    )
    moved = lax.all_to_all(terms, AXES, split_axis=0, concat_axis=0, tiled=True)
    solved = pair_solve(moved)
    returned = lax.all_to_all(solved, AXES, split_axis=0, concat_axis=0, tiled=True)
    return sweeps(returned)


def solution(mesh):
    placed = (
        P(None, AXES, None),
        P(None, AXES, None),
        P(None, AXES, None),
        P(AXES),
        P(AXES),
        P(AXES),
        P(AXES),
        P(None, AXES),
    )
    return jax.shard_map(
        on_device,
        mesh=mesh,
        in_specs=placed,
        out_specs=(P(None, AXES), P(None, AXES)),
        check_vma=False,
    )
```
